32 devices in a mesh: dp: 8 (over z, x), mp: 4 (over y, core).
Axes of the slice: x: 2, y: 2, z: 4, core: 2. Of those that a mesh axis runs over, the one named last changes fastest.
Arguments:
- field_ids: int32 [26, 49152], P(None, 'dp'), may hold values from 0 to 4095
- field_present: int32 [26, 49152], P(None, 'dp'), may hold values 0 or 1
- dense_values: float32 [13, 49152], P(None, ('dp', 'mp')), may hold values from -6 to 6
- dense_present: int32 [13, 49152], P(None, ('dp', 'mp')), may hold values 0 or 1
- clicked: int32 [49152], P(('dp', 'mp')), may hold values 0 or 1
- tables: bfloat16 [4096, 1014], P('mp'), may hold values from -6 to 6
- cross_weight: bfloat16 [1027, 1027], replicated, may hold values from -0.1875 to 0.1875
- cross_bias: float32 [1027], replicated, may hold values from -3 to 3
- deep_weight: bfloat16 [1027, 1024], replicated, may hold values from -0.1875 to 0.1875
- deep_bias: float32 [1024], replicated, may hold values from -3 to 3
- head_cross: float32 [1027], replicated, may hold values from -0.125 to 0.125
- head_deep: float32 [1024], replicated, may hold values from -0.125 to 0.125
- head_bias: float32 [1], replicated, may hold values from -3 to 3
Outputs:
- logits: float32 [49152], P(('dp', 'mp'))
- loss: float32 [], replicated
- dense_grad: float32 [13, 49152], P(None, ('dp', 'mp'))
- tables_grad: float32 [4096, 1014], P(('mp', 'dp'))
- cross_weight_grad: float32 [1027, 1027], replicated
- cross_bias_grad: float32 [1027], replicated
- deep_weight_grad: float32 [1027, 1024], replicated
- deep_bias_grad: float32 [1024], replicated
- head_cross_grad: float32 [1027], replicated
- head_deep_grad: float32 [1024], replicated
- head_bias_grad: float32 [1], replicated
The draws below stay inside these ranges and needn't reach their ends.
All inputs are finite; a program needn't handle non-finite values. No bound on the sum of `field_present` or of `dense_present` or of `clicked` on one device may be relied on, other than what follows from the above.
Results may differ from the reference program's by a relative error of at most 0.002.
Values may be sent and summed in bfloat16 or wider, within the bound.
No kernel may reach another device: no remote copies, remote signals or barrier semaphores. Data moves between devices by JAX's collectives and lax.ppermute only.
A program may use at most 128 MiB of HBM per device.

```python
import math
import jax
import jax.numpy as jnp
import numpy as np
from jax import lax

FIELDS = 26
EMB = 39
DENSE = 13
ROWS = 4096
HIDDEN_SIZE = 1024
BATCH_DP = 6144
CAT = 1014
WIDTH = 1027
EXAMPLES = 49152
N_DP = 8


def set_ends(array, own_key, least, top_value):
    dims = array.shape
    index_at = [jax.random.randint(jax.random.fold_in(own_key, axis), (), 0, dims[axis]) for axis in range(len(dims))]
    array = array.at[tuple(index_at)].set(least)
    longest = dims.index(max(dims))
    index_at[longest] = (index_at[longest] + 1) % dims[longest]
    return array.at[tuple(index_at)].set(top_value)


def block_scale(rng, shape, cuts, smallest, largest):
    loudness = 1.0
    for position, parts in cuts:
        draws = jax.random.uniform(jax.random.fold_in(jax.random.fold_in(rng, 6), position), (parts,), jnp.float32, smallest / len(cuts), largest / len(cuts))
        loudness = loudness * jnp.repeat(jnp.exp(draws), shape[position] // parts).reshape((-1,) + (1,) * (len(shape) - 1 - position))
    return loudness


def cumulative_ranks(number_of, lean):
    loads = [(1 << 20) // math.isqrt(rank ** lean) + 1 for rank in range(1, number_of + 1)]
    width = 1 + sum(loads) // (1 << 30)
    return np.cumsum(np.array([max(1, weight // width) for weight in loads]))


def ranked_ids(rng, shape, count, slope):
    grid = cumulative_ranks(count, slope)
    ticket = jax.random.randint(jax.random.fold_in(rng, 1), shape, 0, int(grid[count - 1]))
    standing = jnp.searchsorted(jnp.asarray(grid, jnp.int32), ticket, side="right")
    return jax.random.permutation(jax.random.fold_in(rng, 2), count)[standing].astype(jnp.int32)


def normal_values(rng, extent, spread, reach, shards=(), kind=jnp.bfloat16):
    level = block_scale(rng, extent, shards, -0.22, 0.18) if shards else 1.0
    result = jax.random.normal(rng, extent, jnp.float32) * spread * level
    return jnp.minimum(jnp.maximum(result, -reach), reach).astype(kind)


def setup_inputs(seed: int = 0) -> dict:
    keys = jax.random.split(jax.random.key(seed), 14)
    return {
        "field_ids": set_ends(ranked_ids(keys[0], (FIELDS, EXAMPLES), ROWS, 2), jax.random.fold_in(keys[0], 3), 0, ROWS - 1).astype(jnp.int32),
        "field_present": set_ends((jax.random.randint(keys[1], (FIELDS, EXAMPLES), 0, 5) < 4).astype(jnp.int32), jax.random.fold_in(keys[1], 1), 0, 1),
        "dense_values": normal_values(keys[2], (DENSE, EXAMPLES), 1.0, 6.0, ((1, 32),), jnp.float32),
        "dense_present": set_ends((jax.random.randint(keys[3], (DENSE, EXAMPLES), 0, 4) < 3).astype(jnp.int32), jax.random.fold_in(keys[3], 1), 0, 1),
        "clicked": set_ends((jax.random.randint(keys[4], (EXAMPLES,), 0, 4) < 1).astype(jnp.int32), jax.random.fold_in(keys[4], 1), 0, 1),
        "tables": normal_values(keys[5], (ROWS, CAT), 1.0, 6.0, ((0, 4),)),
        "cross_weight": normal_values(keys[6], (WIDTH, WIDTH), WIDTH ** -0.5, 0.1875),
        "cross_bias": normal_values(keys[7], (WIDTH,), 0.5, 3.0, (), jnp.float32),
        "deep_weight": normal_values(keys[8], (WIDTH, HIDDEN_SIZE), WIDTH ** -0.5, 0.1875),
        "deep_bias": normal_values(keys[9], (HIDDEN_SIZE,), 0.5, 3.0, (), jnp.float32),
        "head_cross": normal_values(keys[10], (WIDTH,), (WIDTH + HIDDEN_SIZE) ** -0.5, 0.125, (), jnp.float32),
        "head_deep": normal_values(keys[11], (HIDDEN_SIZE,), (WIDTH + HIDDEN_SIZE) ** -0.5, 0.125, (), jnp.float32),
        "head_bias": normal_values(keys[12], (1,), 1.0, 3.0, (), jnp.float32),
    }


@jax.custom_vjp
def low(v):
    return lax.optimization_barrier(v.astype(jnp.bfloat16)).astype(jnp.float32)

@jax.custom_vjp
def low_back(v):
    return v

def low_keep(v):
    return (low(v), None)

def low_pass(kept, grad):
    return (grad,)

def back_keep(v):
    return (v, None)

def back_low(kept, grad):
    return (low(grad),)
low.defvjp(low_keep, low_pass)
low_back.defvjp(back_keep, back_low)

def forward(params, dense_block, chosen, dense_mask, labels):
    tables, cross_weight, cross_bias, deep_weight, deep_bias, head_cross, head_deep, head_bias = params
    count = chosen.shape[1]
    table_three = tables.reshape(ROWS, FIELDS, EMB)
    picked = table_three[chosen.T, jnp.arange(FIELDS)[None, :]]
    embedded = low_back(picked.reshape(count, FIELDS * EMB))
    x_zero = jnp.concatenate([embedded, (dense_block * dense_mask).T], axis=1)
    x_low = low(x_zero)
    cross_pre = low_back(jnp.dot(x_low, cross_weight, precision=lax.Precision.HIGHEST) + cross_bias)
    crossed = x_zero * cross_pre + x_zero
    deep_pre = low_back(jnp.dot(x_low, deep_weight, precision=lax.Precision.HIGHEST) + deep_bias)
    deep_act = jax.nn.gelu(deep_pre, approximate=True)
    logit = jnp.dot(crossed, head_cross, precision=lax.Precision.HIGHEST) + jnp.dot(deep_act, head_deep, precision=lax.Precision.HIGHEST) + head_bias[0]
    loss_sum = jnp.sum(jax.nn.softplus(logit) - labels * logit)
    return (logit, loss_sum)

def reference(field_ids, field_present, dense_values, dense_present, clicked, tables, cross_weight, cross_bias, deep_weight, deep_bias, head_cross, head_deep, head_bias):
    chosen = jnp.where(field_present > 0, field_ids, 0).astype(jnp.int32)
    chosen_blocks = chosen.reshape(FIELDS, N_DP, BATCH_DP).transpose(1, 0, 2)
    dense_blocks = dense_values.astype(jnp.float32).reshape(DENSE, N_DP, BATCH_DP).transpose(1, 0, 2)
    mask_blocks = dense_present.astype(jnp.float32).reshape(DENSE, N_DP, BATCH_DP).transpose(1, 0, 2)
    label_blocks = clicked.astype(jnp.float32).reshape(N_DP, BATCH_DP)
    params = tuple((p.astype(jnp.float32) for p in (tables, cross_weight, cross_bias, deep_weight, deep_bias, head_cross, head_deep, head_bias)))
    scale = 1.0 / math.sqrt(EXAMPLES)

    def step(carry, block):
        ids_block, dense_block, mask_block, label_block = block

        def primal(weights, dense_in):
            return forward(weights, dense_in, ids_block, mask_block, label_block)
        (logit, loss_sum), back = jax.vjp(primal, params, dense_block)
        grads, dense_back = back((jnp.zeros_like(logit), jnp.asarray(scale, dtype=loss_sum.dtype)))
        totals, loss_total = carry
        totals = jax.tree.map(lambda a, b: a + b, totals, grads)
        return ((totals, loss_total + loss_sum), (logit, dense_back))
    init = (jax.tree.map(jnp.zeros_like, params), jnp.zeros((), params[2].dtype))
    (totals, loss_total), (logit_all, dense_all) = lax.scan(step, init, (chosen_blocks, dense_blocks, mask_blocks, label_blocks))
    logits = logit_all.reshape(EXAMPLES)
    dense_grad = dense_all.transpose(1, 0, 2).reshape(DENSE, EXAMPLES)
    loss = loss_total / EXAMPLES
    return (logits, loss, dense_grad, totals[0], totals[1], totals[2], totals[3], totals[4], totals[5], totals[6], totals[7])
```

```python
import math

import jax
import jax.numpy as jnp
from jax import lax
from jax.experimental import pallas as pl
from jax.experimental.pallas import tpu as pltpu
from jax.sharding import PartitionSpec as P

BF16, F32, F16 = jnp.bfloat16, jnp.float32, jnp.float16
HI = 256
FRONT = 8
PAD = 40
TILE = 256
TOP = 32768.0
LIMIT = 60 * 1024 * 1024
GELU_S = math.sqrt(2.0 / math.pi)
GELU_C = 0.044715


def params(**more):
    return pltpu.CompilerParams(vmem_limit_bytes=LIMIT, **more)


def cost(flops, moved):
    return pl.CostEstimate(flops=int(flops), bytes_accessed=int(moved), transcendentals=0)


def ceil_to(value, unit):
    return -(-value // unit) * unit


def dot_nn(left, right):
    return jnp.dot(left, right, preferred_element_type=F32)


def dot_nt(left, right, precision=None):
    return lax.dot_general(
        left, right, (((1,), (1,)), ((), ())), preferred_element_type=F32, precision=precision
    )


def onehot_rows(place, width):
    rows = lax.broadcasted_iota(jnp.int16, (HI, width), 0)
    return jnp.where(rows == place.astype(jnp.int16), jnp.ones((), BF16), jnp.zeros((), BF16))


def lookup_kernel(emb, blocks, hi_ref, lo_ref, *refs):
    sources, out_ref, flat, packed = refs[:4], refs[4], refs[5], refs[6]
    n_fields, examples = hi_ref.shape
    rows = emb * n_fields
    for s, source in enumerate(sources):
        flat[s, 0:rows, :] = source[...].astype(F32)
    for f in range(n_fields):
        for s in range(4):
            for b in range(blocks):
                piece = flat[s, emb * f : emb * f + PAD, b * HI : (b + 1) * HI]
                at = (s * blocks + b) * PAD
                packed[f, at : at + PAD, :] = piece.astype(BF16)

    def step(t, carry):
        at = pl.multiple_of(t * TILE, TILE)
        for f in range(n_fields):
            place = hi_ref[f : f + 1, pl.ds(at, TILE)]
            block = lo_ref[f : f + 1, pl.ds(at, TILE)]
            found = dot_nn(packed[f], onehot_rows(place, TILE))
            acc = found[0:PAD]
            for b in range(1, 4 * blocks):
                acc = jnp.where(block == b, found[b * PAD : (b + 1) * PAD], acc)
            out_ref[f, :, pl.ds(at, TILE)] = acc
        return carry

    lax.fori_loop(0, examples // TILE, step, 0)


def lookup(hi, lo, sources, emb):
    n_fields, examples = hi.shape
    rows, width = sources[0].shape
    blocks = width // HI
    n_rows = 4 * blocks * PAD
    return pl.pallas_call(
        lambda *refs: lookup_kernel(emb, blocks, *refs),
        out_shape=jax.ShapeDtypeStruct((n_fields, PAD, examples), F32),
        scratch_shapes=[
            pltpu.VMEM((4, ceil_to(rows, 8) + 8, width), F32),
            pltpu.VMEM((n_fields, n_rows, HI), BF16),
        ],
        compiler_params=params(),
        cost_estimate=cost(2 * n_fields * n_rows * HI * examples, 4 * n_fields * PAD * examples),
        name="lookup",
    )(hi, lo, *sources)


def wide(column, width):
    return jnp.concatenate([column] * (width // 128), axis=1)


def fold(values):
    total = values[:, 0:128]
    for at in range(128, values.shape[1], 128):
        total = total + values[:, at : at + 128]
    return total


def layers_kernel(sizes, scale, *refs):
    fields, emb, dense, n_chunks = sizes
    chunks = refs[:n_chunks]
    (dv_ref, dm_ref, lab_ref, wt_ref, w_ref, dwt_ref, dw_ref, cb_ref, db_ref, hc_ref, hd_ref, hb_ref) = refs[
        n_chunks : n_chunks + 12
    ]
    (logit_ref, xa_ref, dc_ref, dd_ref, demb_ref, dg_ref, hca_ref, hda_ref, sc_ref) = refs[
        n_chunks + 12 : n_chunks + 21
    ]
    x_ref, cp_ref, dp_ref = refs[n_chunks + 21 :]
    rows, width = x_ref.shape
    cat = fields * emb
    full = cat + dense
    hidden = dp_ref.shape[0]
    step = 128
    cuts = [(a, min(a + step, rows)) for a in range(0, rows, step)]
    hid_cuts = [(a, min(a + step, hidden)) for a in range(0, hidden, step)]

    @pl.when(pl.program_id(0) == 0)
    def _():
        hca_ref[...] = jnp.zeros_like(hca_ref)
        hda_ref[...] = jnp.zeros_like(hda_ref)
        sc_ref[...] = jnp.zeros_like(sc_ref)

    f = 0
    for chunk in chunks:
        for k in range(chunk.shape[0]):
            x_ref[emb * f : emb * f + PAD, :] = chunk[k]
            f += 1
    x_ref[cat:full, :] = dv_ref[...] * dm_ref[...].astype(F32)
    x_ref[full:rows, :] = jnp.zeros((rows - full, width), F32)
    x_low = x_ref[...].astype(BF16)
    tail = xa_ref.shape[0] - (cat // 16) * 16
    base = xa_ref.shape[0] - tail
    xa_ref[0:base, :] = x_low[0:base]
    last = jnp.concatenate([x_ref[base:rows, :], jnp.zeros((base + tail - rows, width), F32)], axis=0)
    index = lax.broadcasted_iota(jnp.int32, (tail, width), 0) + base
    xa_ref[base:, :] = jnp.where(index == full, 1.0, last).astype(BF16)

    cp_ref[...] = dot_nn(wt_ref[...], x_low)
    dp_ref[...] = dot_nn(dwt_ref[...], x_low)
    logit = jnp.zeros((8, width), F32)
    for a, b in cuts:
        x = x_ref[a:b, :]
        cp = cp_ref[a:b, :] + wide(cb_ref[a:b, :], width)
        cp_ref[a:b, :] = cp
        term = (x * cp + x) * wide(hc_ref[a:b, :], width)
        for r in range(0, b - a, 8):
            logit = logit + term[r : r + 8]
    for a, b in hid_cuts:
        v = dp_ref[a:b, :] + wide(db_ref[a:b, :], width)
        dp_ref[a:b, :] = v
        act = 0.5 * v * (1.0 + jnp.tanh(GELU_S * (v + GELU_C * v * v * v)))
        term = act * wide(hd_ref[a:b, :], width)
        for r in range(0, b - a, 8):
            logit = logit + term[r : r + 8]
    logit = jnp.sum(logit, axis=0, keepdims=True) + hb_ref[0:1, 0:1]
    logit_ref[...] = logit
    labels = lab_ref[...].astype(F32)
    small = jnp.exp(-jnp.abs(logit))
    loss = jnp.maximum(logit, 0.0) + jnp.log1p(small) - labels * logit
    sig = jnp.where(logit >= 0.0, 1.0, small) / (1.0 + small)
    dlogit = (sig - labels) * scale
    sc_ref[0:1, :] += fold(loss)
    sc_ref[1:2, :] += fold(dlogit)

    for a, b in cuts:
        x = x_ref[a:b, :]
        cp = cp_ref[a:b, :]
        hca_ref[a:b, :] += fold(dlogit * (x * cp + x))
        dcrossed = dlogit * wide(hc_ref[a:b, :], width)
        dc_ref[a:b, :] = (dcrossed * x).astype(BF16)
        cp_ref[a:b, :] = dcrossed * (cp + 1.0)
    if dc_ref.shape[0] > rows:
        dc_ref[rows:, :] = jnp.zeros((dc_ref.shape[0] - rows, width), BF16)
    for a, b in hid_cuts:
        v = dp_ref[a:b, :]
        t = jnp.tanh(GELU_S * (v + GELU_C * v * v * v))
        half = 0.5 * (1.0 + t)
        hda_ref[a:b, :] += fold(dlogit * (v * half))
        slope = half + 0.5 * v * (1.0 - t * t) * (GELU_S * (1.0 + 3.0 * GELU_C * v * v))
        dd_ref[a:b, :] = (dlogit * wide(hd_ref[a:b, :], width) * slope).astype(BF16)
    x_ref[...] = (
        cp_ref[...] + dot_nn(w_ref[...], dc_ref[0:rows, :]) + dot_nn(dw_ref[...], dd_ref[...])
    )
    for f in range(fields):
        demb_ref[f] = x_ref[emb * f : emb * f + PAD, :].astype(BF16)
    dg_ref[...] = x_ref[cat:full, :] * dm_ref[...].astype(F32)


def layers(chunks, dense_values, dense_present, labels, weights, columns, emb, scale):
    wt, w, dwt, dw = weights
    fields = sum(c.shape[0] for c in chunks)
    dense, examples = dense_values.shape
    rows, hidden = w.shape[0], dw.shape[1]
    tall = ceil_to(rows, 16)
    column = lambda r: pl.BlockSpec((r, TILE), lambda t: (0, t))
    whole = lambda a: pl.BlockSpec(a.shape, lambda t: (0,) * a.ndim, pipeline_mode=pl.Buffered(1))
    kept = lambda r: pl.BlockSpec((r, 128), lambda t: (0, 0))
    shape = jax.ShapeDtypeStruct
    return pl.pallas_call(
        lambda *refs: layers_kernel((fields, emb, dense, len(chunks)), scale, *refs),
        grid=(examples // TILE,),
        in_specs=[pl.BlockSpec((c.shape[0], PAD, TILE), lambda t: (0, 0, t)) for c in chunks]
        + [column(dense), column(dense), column(1)]
        + [whole(a) for a in (wt, w, dwt, dw, *columns)],
        out_specs=[
            column(1),
            column(tall),
            column(tall),
            column(hidden),
            pl.BlockSpec((fields, PAD, TILE), lambda t: (0, 0, t)),
            column(dense),
            kept(rows),
            kept(hidden),
            kept(8),
        ],
        out_shape=[
            shape((1, examples), F32),
            shape((tall, examples), BF16),
            shape((tall, examples), BF16),
            shape((hidden, examples), BF16),
            shape((fields, PAD, examples), BF16),
            shape((dense, examples), F32),
            shape((rows, 128), F32),
            shape((hidden, 128), F32),
            shape((8, 128), F32),
        ],
        scratch_shapes=[
            pltpu.VMEM((rows, TILE), F32),
            pltpu.VMEM((rows, TILE), F32),
            pltpu.VMEM((hidden, TILE), F32),
        ],
        compiler_params=params(),
        cost_estimate=cost(2 * examples * rows * (2 * rows + 2 * hidden), 9 * 2**20 + 20 * rows * examples),
        name="layers",
    )(*chunks, dense_values, dense_present, labels, wt, w, dwt, dw, *columns)


def weight_kernel(rows, full, examples_all, xa_ref, xb_ref, dc_ref, dct_ref, dd_ref, hc_ref, hct_ref, hd_ref, sc_ref, out_ref, top_ref):
    quarter = out_ref.shape[3] - FRONT
    core = pl.program_id(0) // (pl.num_programs(0) // 2)
    x = xa_ref[0:rows, :]
    deep = dot_nt(x, dd_ref[...])
    cross = dot_nt(x, dc_ref[...])
    tail = dct_ref[...]
    over = dot_nt(tail, xb_ref[...])[0:8]
    corner = dot_nt(tail, xa_ref[xa_ref.shape[0] - 16 :, :])
    ones = jnp.ones((8, 128), F32)
    total = lambda ref: dot_nt(ones, ref[...], lax.Precision.HIGHEST)
    row = lax.broadcasted_iota(jnp.int32, (8, TILE), 0)
    first = pl.program_id(0) == 0
    heads = jnp.where(row == 0, total(hc_ref), jnp.where(row == 1, total(hd_ref), 0.0))
    spare = jnp.concatenate([corner[0:8], jnp.zeros((8, TILE - 16), F32)], axis=1)
    spare = jnp.concatenate([jnp.zeros((2, TILE), F32), spare[0:3], jnp.zeros((3, TILE), F32)], axis=0)
    ends = total(hct_ref)
    ends = jnp.concatenate([ends, jnp.zeros((8, TILE - 8), F32)], axis=1)
    sums = jnp.sum(sc_ref[...], axis=1, keepdims=True)
    lane = lax.broadcasted_iota(jnp.int32, (8, TILE), 1)
    scalars = jnp.where(lane == 0, sums[0:1] / examples_all, jnp.where(lane == 1, sums[1:2], 0.0))
    small = spare + jnp.where(row == 5, ends, 0.0) + jnp.where(row == 6, scalars, 0.0)
    heads = heads + jnp.where(first, small, 0.0)
    parts = [(0, deep), (rows, cross), (2 * rows, over), (2 * rows + 8, heads)]
    top = jnp.zeros((8, TILE), F32)
    for base, part in parts:
        for r in range(0, part.shape[0], 8):
            top = jnp.maximum(top, jnp.abs(part[r : r + 8]))
    top = jnp.maximum(top[:, 0:128], top[:, 128:256])

    @pl.when(first)
    def _():
        top_ref[...] = top

    @pl.when(jnp.logical_not(first))
    def _():
        top_ref[...] = jnp.maximum(top_ref[...], top)

    for base, part in parts:
        at = 0
        while at < part.shape[0]:
            q, r = divmod(base + at, quarter)
            n = min(part.shape[0] - at, quarter - r)
            place = jnp.where(core == 0, (0, 2, 1, 3)[q], q)
            for h in range(2):
                out_ref[0, place, h, FRONT + r : FRONT + r + n, :] = part[at : at + n, h * 128 : (h + 1) * 128]
            at += n


def weight_grads(xa, dc, dd, hca, hda, sc, full, examples_all):
    tall, examples = xa.shape
    rows, hidden = hca.shape[0], hda.shape[0]
    quarter = ceil_to(2 * rows + 16, 32) // 4
    return pl.pallas_call(
        lambda *refs: weight_kernel(rows, full, examples_all, *refs),
        grid=(hidden // TILE,),
        in_specs=[
            pl.BlockSpec((tall, examples), lambda j: (0, 0), pipeline_mode=pl.Buffered(1)),
            pl.BlockSpec((TILE, examples), lambda j: (j, 0)),
            pl.BlockSpec((TILE, examples), lambda j: (j, 0)),
            pl.BlockSpec((16, examples), lambda j: (hidden // 16, 0)),
            pl.BlockSpec((TILE, examples), lambda j: (j, 0)),
            pl.BlockSpec((TILE, 128), lambda j: (j, 0)),
            pl.BlockSpec((8, 128), lambda j: (hidden // 8, 0)),
            pl.BlockSpec((TILE, 128), lambda j: (j, 0)),
            pl.BlockSpec((8, 128), lambda j: (0, 0)),
        ],
        out_specs=[
            pl.BlockSpec((1, 4, 2, FRONT + quarter, 128), lambda j: (j // 2, 0, j % 2, 0, 0)),
            pl.BlockSpec((8, 128), lambda j: (0, 0)),
        ],
        out_shape=[
            jax.ShapeDtypeStruct((2, 4, hidden // 256, FRONT + quarter, 128), F32),
            jax.ShapeDtypeStruct((8, 128), F32),
        ],
        compiler_params=params(),
        cost_estimate=cost(4 * examples * rows * hidden, 20 * rows * hidden),
        name="weight_grads",
    )(xa, xa, dc, dc, dd, hca, hca, hda, sc)


def spread_kernel(hi_ref, lo_ref, own_ref, sib_ref, out_ref, top_ref, sel, hot):
    n_blocks = out_ref.shape[0] * out_ref.shape[1]
    examples = own_ref.shape[2]
    for s, ref in enumerate((own_ref, sib_ref)):
        for at in range(0, examples, TILE):
            place = hi_ref[0, s : s + 1, at : at + TILE]
            block = lo_ref[0, s : s + 1, at : at + TILE]
            grads = ref[0, :, at : at + TILE].astype(F32)
            cols = slice(s * examples + at, s * examples + at + TILE)
            sel[:, cols] = jnp.concatenate(
                [jnp.where(block == b, grads, 0.0) for b in range(n_blocks)], axis=0
            ).astype(BF16)
            hot[:, cols] = onehot_rows(place, TILE)
    sums = dot_nt(sel[...], hot[...])
    top = jnp.zeros((8, HI), F32)
    for r in range(0, sums.shape[0], 8):
        top = jnp.maximum(top, jnp.abs(sums[r : r + 8]))
    top = jnp.maximum(top[:, 0:128], top[:, 128:256])

    @pl.when(pl.program_id(0) == 0)
    def _():
        top_ref[...] = top

    @pl.when(pl.program_id(0) != 0)
    def _():
        top_ref[...] = jnp.maximum(top_ref[...], top)

    for b in range(n_blocks):
        for h in range(2):
            out_ref[b // out_ref.shape[1], b % out_ref.shape[1], h] = sums[
                b * PAD : (b + 1) * PAD, h * 128 : (h + 1) * 128
            ]


def spread(hi, lo, own, sib, first, count, blocks):
    fields, _, examples = own.shape
    return pl.pallas_call(
        spread_kernel,
        grid=(count,),
        in_specs=[pl.BlockSpec((1, 2, examples), lambda f: (f + first, 0, 0))] * 2
        + [pl.BlockSpec((1, PAD, examples), lambda f: (f + first, 0, 0))] * 2,
        out_specs=[
            pl.BlockSpec((2, blocks, 2, PAD, 128), lambda f: (0, 0, 0, f, 0)),
            pl.BlockSpec((8, 128), lambda f: (0, 0)),
        ],
        out_shape=[
            jax.ShapeDtypeStruct((2, blocks, 2, count * PAD, 128), F32),
            jax.ShapeDtypeStruct((8, 128), F32),
        ],
        scratch_shapes=[
            pltpu.VMEM((2 * blocks * PAD, 2 * examples), BF16),
            pltpu.VMEM((HI, 2 * examples), BF16),
        ],
        compiler_params=params(),
        cost_estimate=cost(8 * count * blocks * PAD * HI * examples, 4 * count * PAD * 16 * 128 * blocks),
        name="spread",
    )(hi, lo, own, sib)


def flip(array, axis, bit):
    size = lax.axis_size(axis)
    return lax.ppermute(array, axis, [(i, i ^ (1 << bit)) for i in range(size)])


def bit_of(axis, bit):
    return (lax.axis_index(axis) >> bit) & 1


def crossed_pairs(stage, n_dp, n_mp):
    pairs = []
    for d in range(n_dp):
        for m in range(n_mp):
            along_dp = (m & 1) == stage
            to = (d ^ 1, m) if along_dp else (d, m ^ 2)
            pairs.append((d * n_mp + m, to[0] * n_mp + to[1]))
    return pairs


def crossed_flip(array, stage):
    return lax.ppermute(array, ("dp", "mp"), crossed_pairs(stage, lax.axis_size("dp"), lax.axis_size("mp")))


def crossed_bit(stage):
    return jnp.where(bit_of("mp", 0) == stage, bit_of("dp", 0), bit_of("mp", 1))


def exponent_of(top):
    top = jnp.maximum(jnp.max(top, axis=(0, 1), keepdims=True)[0], 1e-30)
    return jnp.broadcast_to(jnp.ceil(jnp.log2(top)) - 14.0, (128,))


def halve(acc, expo, mine, send, at):
    away = lax.dynamic_index_in_dim(acc, 1 - mine, 0, keepdims=False)
    kept = lax.dynamic_index_in_dim(acc, mine, 0, keepdims=False)
    row = lax.broadcasted_iota(jnp.int32, away.shape, away.ndim - 2)
    here = expo.reshape((1,) * (away.ndim - 1) + (128,))
    message = jnp.where(row == at, here, away * jnp.exp2(-here)).astype(F16)
    got = send(message)
    theirs = got[(0,) * (got.ndim - 2) + (at,)].astype(F32)
    acc = kept + got.astype(F32) * jnp.exp2(theirs).reshape(here.shape[: got.ndim])
    return acc, jnp.maximum(expo, theirs) + 1.0


def double(piece, mine, send):
    other = send(piece)
    low = mine == 0
    return jnp.stack([jnp.where(low, piece, other), jnp.where(low, other, piece)], axis=0)


def stages():
    return [
        (crossed_bit(0), lambda a: crossed_flip(a, 0)),
        (crossed_bit(1), lambda a: crossed_flip(a, 1)),
        (bit_of("dp", 1), lambda a: flip(a, "dp", 1)),
        (bit_of("dp", 2), lambda a: flip(a, "dp", 2)),
    ]


def assemble_kernel(rows, full, hidden, step_cols, in_ref, over_ref, cross_ref, deep_ref, vec_ref):
    t = pl.program_id(0)
    last = pl.num_programs(0) - 1
    core = t // (step_cols // 2)
    quarter = in_ref.shape[4] - FRONT
    parts = []
    for r in range(4):
        q = jnp.where(core == 0, (0, 2, 1, 3)[r], r)
        parts.append(in_ref[0, q // 2, q % 2, 0, FRONT:, :])
    every = jnp.concatenate(parts, axis=0)

    @pl.when(t < last)
    def _():
        deep_ref[...] = every[0:full]
        cross_ref[...] = every[rows : rows + full]
        vec_ref[0:1, :] = every[rows + full : rows + full + 1]
        vec_ref[1:2, :] = every[full : full + 1]
        vec_ref[2:4, :] = every[2 * rows + 8 : 2 * rows + 10]
        vec_ref[4:8, :] = every[2 * rows + 12 : 2 * rows + 16]

    @pl.when(t == last)
    def _():
        cross_ref[...] = over_ref[0:full, :]


def assemble(pieces, rows, full, hidden):
    cols = hidden // 128
    quarter = pieces.shape[4] - FRONT
    z = cols // 2
    spare = pieces[:, 1, 1, :, FRONT + quarter - 16 :, :].transpose(2, 0, 1, 3).reshape(16, hidden)
    extra = full - hidden
    over = jnp.concatenate([spare[0:8], jnp.zeros((8, 128), F32)], axis=1)[0:extra]
    over = lax.dynamic_update_slice(over, spare[10 : 10 + extra, 0 : rows - hidden], (0, hidden))[:, 0:rows]
    over = jnp.pad(over.T, ((0, 0), (0, 128 - extra)))
    return pl.pallas_call(
        lambda *refs: assemble_kernel(rows, full, hidden, cols, *refs),
        grid=(cols + 1,),
        in_specs=[
            pl.BlockSpec(
                (1, 2, 2, 1, FRONT + quarter, 128),
                lambda t: (jnp.minimum(t, cols - 1) // z, 0, 0, jnp.minimum(t, cols - 1) % z, 0, 0),
            ),
            pl.BlockSpec((rows, 128), lambda t: (0, 0)),
        ],
        out_specs=[
            pl.BlockSpec((full, 128), lambda t: (0, t)),
            pl.BlockSpec((full, 128), lambda t: (0, jnp.minimum(t, cols - 1))),
            pl.BlockSpec((8, 128), lambda t: (0, jnp.minimum(t, cols - 1))),
        ],
        out_shape=[
            jax.ShapeDtypeStruct((full, full), F32),
            jax.ShapeDtypeStruct((full, hidden), F32),
            jax.ShapeDtypeStruct((8, hidden), F32),
        ],
        compiler_params=params(),
        cost_estimate=cost(0, 16 * rows * hidden),
        name="assemble",
    )(pieces, over), over


def table_place(ids, table_rows, n_dp, core):
    upper = ids // (2 * table_rows)
    rest = ids % table_rows
    if n_dp == 8:
        piece = table_rows // n_dp
        at = rest // piece
        low = at % 2
        first = jnp.where(core == 0, low, upper)
        second = jnp.where(core == 0, upper, low)
        block = first * 4 + second * 2 + at // 4
        place = (at // 2) % 2 * piece + rest % piece
    else:
        block = upper * (table_rows // HI) + rest // HI
        place = rest % HI
    return place, jnp.where((ids // table_rows) % 2 == core, block, -1)


def body(
    field_ids,
    field_present,
    dense_values,
    dense_present,
    clicked,
    tables,
    cross_weight,
    cross_bias,
    deep_weight,
    deep_bias,
    head_cross,
    head_deep,
    head_bias,
):
    fields, batch_group = field_ids.shape
    table_rows, cat = tables.shape
    emb = cat // fields
    full, hidden = deep_weight.shape
    dense = full - cat
    n_dp, n_mp = lax.axis_size("dp"), lax.axis_size("mp")
    examples = batch_group // n_mp
    examples_all = batch_group * n_dp
    blocks = table_rows // HI
    rows = ceil_to(full + 1, 8)
    me = lax.axis_index("mp")
    core = me & 1

    columns = tables.T
    ends = [0, 8, 16, 24, fields]
    direct = [(d * n_mp + m, d * n_mp + (m ^ 2)) for d in range(n_dp) for m in range(n_mp) if (m & 1) == (d & 1)]
    relay = [(d * n_mp + m, (d ^ 1) * n_mp + m) for d in range(n_dp) for m in range(n_mp) if (m & 1) == (d & 1)]
    is_direct = core == bit_of("dp", 0)
    mine, near, far, far_near = [], [], [], []
    for a, b in zip(ends[:-1], ends[1:]):
        mine.append(columns[a * emb : b * emb])
    for part in mine:
        got = lax.ppermute(part, ("dp", "mp"), direct)
        far.append(jnp.where(is_direct, got, lax.ppermute(got, ("dp", "mp"), relay)))
    for part in mine:
        near.append(flip(part, "mp", 0))
    for part in far:
        far_near.append(flip(part, "mp", 0))

    chosen = jnp.where(field_present > 0, field_ids, 0)
    own_ids = lax.dynamic_slice_in_dim(chosen, me * examples, examples, 1)
    sib_ids = lax.dynamic_slice_in_dim(chosen, (me ^ 1) * examples, examples, 1)
    hi_own = own_ids & (HI - 1)
    lo_own = (own_ids // HI) ^ (me * blocks)
    pair_ids = jnp.stack([own_ids, sib_ids], axis=1)
    hi_pair, lo_pair = table_place(pair_ids, table_rows, n_dp, core)

    pad_in = rows - full
    w = jnp.pad(cross_weight, ((0, pad_in), (0, pad_in)))
    dw = jnp.pad(deep_weight, ((0, pad_in), (0, 0)))
    weights = (w.T, w, dw.T, dw)
    spread_out = lambda v, n: jnp.broadcast_to(jnp.pad(v, (0, n - v.shape[0]))[:, None], (n, 128))
    vectors = (
        spread_out(cross_bias, rows),
        spread_out(deep_bias, hidden),
        spread_out(head_cross, rows),
        spread_out(head_deep, hidden),
        spread_out(head_bias, 8),
    )

    chunks = []
    for k, (a, b) in enumerate(zip(ends[:-1], ends[1:])):
        ids = hi_own[a:b], lo_own[a:b]
        if chunks:
            ids, chunks[-1] = lax.optimization_barrier((ids, chunks[-1]))
        chunks.append(lookup(*ids, (mine[k], near[k], far[k], far_near[k]), emb))

    logit, xa, dc, dd, demb, dense_grad, hca, hda, sc = layers(
        chunks,
        dense_values,
        dense_present,
        clicked[None, :],
        weights,
        vectors,
        emb,
        1.0 / math.sqrt(examples_all),
    )
    demb_sib = flip(demb, "mp", 0)
    sums, top = weight_grads(xa, dc, dd, hca, hda, sc, full, examples_all)
    halves = [(0, 13), (13, fields)]
    table_parts = [spread(hi_pair, lo_pair, demb, demb_sib, a, b - a, blocks) for a, b in halves]

    if n_dp == 8:
        part, expo = halve(sums, exponent_of(top), core, lambda a: flip(a, "mp", 0), FRONT - 1)
        part = part.reshape(2, 2, *part.shape[1:])
        for k, (mine_bit, send) in enumerate(stages()):
            if k == 2:
                part = part.reshape(2, 2, *part.shape[1:])
                part = jnp.swapaxes(part, 0, 1)
            part, expo = halve(part, expo, mine_bit, send, FRONT - 1)
        scale = expo[None, :]
        part = (part * jnp.exp2(-scale)).astype(F16)
        for mine_bit, send in reversed(stages()):
            part = double(part, mine_bit, send)
        part = double(part, core, lambda a: flip(a, "mp", 0))
        part = part.astype(F32) * jnp.exp2(scale)
        pieces = jnp.swapaxes(part, 3, 4).reshape(2, 2, 2, hidden // 256, *part.shape[5:])
        table_out = []
        for part, top in table_parts:
            expo = exponent_of(top)
            part = part.reshape(2, 2, 2, 2, *part.shape[3:])
            for k, (mine_bit, send) in enumerate(stages()):
                if k == 2:
                    part = jnp.swapaxes(part, 0, 1)
                part, expo = halve(part, expo, mine_bit, send, PAD - 1)
            table_out.append(part)
        table_out = jnp.concatenate(table_out, axis=0)
    else:
        pieces = lax.psum(sums, ("dp", "mp")).reshape(2, 2, 2, *sums.shape[2:])
        table_out = jnp.concatenate([part for part, _ in table_parts], axis=3)
        table_out = table_out.transpose(0, 3, 1, 2, 4).reshape(2, fields * PAD, table_rows)
        upper = bit_of("mp", 1)
        away = lax.dynamic_index_in_dim(table_out, 1 - upper, 0, keepdims=False)
        table_out = lax.dynamic_index_in_dim(table_out, upper, 0, keepdims=False) + flip(away, "mp", 1)
        table_out = lax.psum_scatter(table_out, "dp", scatter_dimension=1, tiled=True)
    tables_grad = table_out.reshape(fields, PAD, -1)[:, :emb].reshape(cat, -1).T
    (cross_grad, deep_grad, small), over = assemble(pieces, rows, full, hidden)
    return (
        logit[0],
        small[6, 0],
        dense_grad,
        tables_grad,
        cross_grad,
        jnp.concatenate([small[0], over[full, 0 : full - hidden]]),
        deep_grad,
        small[1],
        jnp.concatenate([small[2], small[5, 0 : full - hidden]]),
        small[3],
        small[6, 1:2],
    )


def solution(mesh):
    placed = (
        P(None, "dp"),
        P(None, "dp"),
        P(None, ("dp", "mp")),
        P(None, ("dp", "mp")),
        P(("dp", "mp")),
        P("mp", None),
        P(),
        P(),
        P(),
        P(),
        P(),
        P(),
        P(),
    )
    return jax.shard_map(
        body,
        mesh=mesh,
        in_specs=placed,
        out_specs=(
            P(("dp", "mp")),
            P(),
            P(None, ("dp", "mp")),
            P(("mp", "dp"), None),
            P(),
            P(),
            P(),
            P(),
            P(),
            P(),
            P(),
        ),
        check_vma=False,
    )
```

```python
import math

import jax
import jax.numpy as jnp
from jax import lax
from jax.experimental import pallas as pl
from jax.experimental.pallas import tpu as pltpu
from jax.sharding import PartitionSpec as P

BF16, F32, F16 = jnp.bfloat16, jnp.float32, jnp.float16
HI = 256
SLOPE_TOP = 1.25
X_TOP = 6.0
FRONT = 8
PAD = 40
TILE = 256
WIDE = 512
GELU_S = math.sqrt(2.0 / math.pi)
GELU_C = 0.044715


def params(mebibytes):
    return pltpu.CompilerParams(vmem_limit_bytes=mebibytes * 1024 * 1024)


def cost(flops, moved):
    return pl.CostEstimate(flops=int(flops), bytes_accessed=int(moved), transcendentals=0)


def in_hbm(array):
    return pltpu.with_memory_space_constraint(array, pltpu.HBM)


def ceil_to(value, unit):
    return -(-value // unit) * unit


def dot_nn(left, right):
    return jnp.dot(left, right, preferred_element_type=F32)


def dot_nt(left, right, precision=None):
    return lax.dot_general(
        left, right, (((1,), (1,)), ((), ())), preferred_element_type=F32, precision=precision
    )


def onehot_rows(place, width):
    rows = lax.broadcasted_iota(jnp.int16, (HI, width), 0)
    return jnp.where(rows == place.astype(jnp.int16), jnp.ones((), BF16), jnp.zeros((), BF16))


def prepare_kernel(cw_ref, dw_ref, cb_ref, db_ref, hc_ref, hd_ref, ww_ref, wb_ref, cbo_ref, dbo_ref, hco_ref, hdo_ref, pad):
    full, hidden = dw_ref.shape
    rows = wb_ref.shape[0]
    pad[...] = jnp.zeros_like(pad)
    for source, base, width in ((dw_ref, 0, hidden), (cw_ref, hidden, full)):
        pad[0:full, 0:width] = source[...].astype(F32)
        if width < rows:
            pad[:, width:] = jnp.zeros((pad.shape[0], pad.shape[1] - width), F32)
        wide_width = hidden if base == 0 else rows
        wb_ref[:, base : base + wide_width] = pad[0:rows, 0:wide_width].astype(BF16)
        for r in range(0, wide_width, 128):
            n = min(128, wide_width - r)
            turned = pad[:, r : r + 128].T
            ww_ref[base + r : base + r + n, :] = turned[0:n, 0:rows].astype(BF16)
    for source, out, more in ((cb_ref, cbo_ref, 1.0), (db_ref, dbo_ref, 0.0), (hc_ref, hco_ref, 0.0), (hd_ref, hdo_ref, 0.0)):
        for r in range(0, out.shape[0], 128):
            n = min(128, out.shape[0] - r)
            line = source[:, r : r + 128]
            out[r : r + n, :] = (jnp.broadcast_to(line, (128, 128)).T + more)[0:n]


def prepare(cross_weight, deep_weight, cross_bias, deep_bias, head_cross, head_deep, rows):
    full, hidden = deep_weight.shape
    wide_rows = ceil_to(rows, 128)
    line = lambda v: jnp.pad(v, (0, ceil_to(v.shape[0], 128) - v.shape[0]))[None, :]
    shape = jax.ShapeDtypeStruct
    return pl.pallas_call(
        prepare_kernel,
        out_shape=[
            shape((hidden + rows, rows), BF16),
            shape((rows, hidden + rows), BF16),
            shape((rows, 128), F32),
            shape((hidden, 128), F32),
            shape((rows, 128), F32),
            shape((hidden, 128), F32),
        ],
        scratch_shapes=[pltpu.VMEM((wide_rows, wide_rows), F32)],
        compiler_params=params(16),
        cost_estimate=cost(0, 16 * rows * rows),
        name="prepare",
    )(cross_weight, deep_weight, line(cross_bias), line(deep_bias), line(head_cross), line(head_deep))


def lookup_kernel(emb, blocks, at_row, place_ref, block_ref, *refs):
    sources, out_ref, flat, packed = refs[0:4], refs[4], refs[5], refs[6]
    n_fields, examples = place_ref.shape
    rows = emb * n_fields
    for s, source in enumerate(sources):
        first = at_row if s < 2 else 0
        flat[s, 0:rows, :] = source[first : first + rows, :].astype(F32)
    for f in range(n_fields):
        for s in range(4):
            for b in range(blocks):
                piece = flat[s, emb * f : emb * f + PAD, b * HI : (b + 1) * HI]
                at = (s * blocks + b) * PAD
                packed[f, at : at + PAD, :] = piece.astype(BF16)

    def step(t, carry):
        at = pl.multiple_of(t * WIDE, WIDE)
        for f in range(n_fields):
            place = place_ref[f : f + 1, pl.ds(at, WIDE)]
            block = block_ref[f : f + 1, pl.ds(at, WIDE)]
            found = dot_nn(packed[f], onehot_rows(place, WIDE))
            acc = found[0:PAD]
            for b in range(1, 4 * blocks):
                acc = jnp.where(block == b, found[b * PAD : (b + 1) * PAD], acc)
            out_ref[f, :, pl.ds(at, WIDE)] = acc.astype(BF16)
        return carry

    lax.fori_loop(0, examples // WIDE, step, 0)


def lookup(place, block, sources, at_row, emb):
    n_fields, examples = place.shape
    width = sources[0].shape[1]
    blocks = width // HI
    n_rows = 4 * blocks * PAD
    return pl.pallas_call(
        lambda *refs: lookup_kernel(emb, blocks, at_row, *refs),
        out_shape=jax.ShapeDtypeStruct((n_fields, PAD, examples), BF16),
        scratch_shapes=[
            pltpu.VMEM((4, ceil_to(n_fields * emb, 8) + 8, width), F32),
            pltpu.VMEM((n_fields, n_rows, HI), BF16),
        ],
        compiler_params=params(16),
        cost_estimate=cost(2 * n_fields * n_rows * HI * examples, 4 * n_fields * PAD * examples),
        name="lookup",
    )(place, block, *sources)


def wide(column, width):
    return jnp.concatenate([column] * (width // 128), axis=1)


def fold(values):
    total = values[:, 0:128]
    for at in range(128, values.shape[1], 128):
        total = total + values[:, at : at + 128]
    return total


def peak(top, values):
    for r in range(0, values.shape[0], 8):
        top = jnp.maximum(top, jnp.abs(values[r : r + 8]))
    return top


def exponents(top):
    most = jnp.max(jnp.max(top, axis=1, keepdims=True), axis=0, keepdims=True)
    return jnp.broadcast_to(jnp.ceil(jnp.log(jnp.maximum(most, 1e-30)) * (1.0 / math.log(2.0))) - 14.0, (8, 128))


def layers_kernel(sizes, scale, *refs):
    fields, emb, dense, n_chunks, tiles = sizes
    chunks = refs[:n_chunks]
    (dv_ref, dm_ref, lab_ref, ww_ref, wb_ref, cb_ref, db_ref, hc_ref, hd_ref, hb_ref) = refs[n_chunks : n_chunks + 10]
    (logit_ref, xa_ref, grad_ref, demb_ref, dg_ref, hca_ref, hda_ref, sc_ref, expo_ref) = refs[
        n_chunks + 10 : n_chunks + 19
    ]
    top_ref, wws_ref, wbs_ref, sems, *scratch = refs[n_chunks + 19 :]
    loads = [
        pltpu.make_async_copy(ww_ref, wws_ref, sems.at[0]),
        pltpu.make_async_copy(wb_ref, wbs_ref, sems.at[1]),
    ]
    start = pl.program_id(0) == 0
    hidden = hda_ref.shape[0]
    rows = hca_ref.shape[0]
    width = TILE
    cat = fields * emb
    full = cat + dense
    step = 128
    cuts = [(a, min(a + step, rows)) for a in range(0, rows, step)]
    hid_cuts = [(a, min(a + step, hidden)) for a in range(0, hidden, step)]
    cols = [slice(k * TILE, (k + 1) * TILE) for k in range(tiles)]
    tall = xa_ref.shape[0]

    @pl.when(start)
    def _():
        for load in loads:
            load.start()
        hca_ref[...] = jnp.zeros_like(hca_ref)
        hda_ref[...] = jnp.zeros_like(hda_ref)
        sc_ref[...] = jnp.zeros_like(sc_ref)
        top_ref[...] = jnp.zeros_like(top_ref)

    def gather(k):
        x_ref = scratch[4 * k]
        f = 0
        for chunk in chunks:
            for c in range(chunk.shape[0]):
                x_ref[emb * f : emb * f + PAD, :] = chunk[c, :, cols[k]].astype(F32)
                f += 1
        x_ref[cat:full, :] = dv_ref[:, cols[k]] * dm_ref[:, cols[k]].astype(F32)
        x_ref[full:tall, :] = (
            lax.broadcasted_iota(jnp.int32, (tall - full, width), 0) == 0
        ).astype(F32)
        xa_ref[:, cols[k]] = x_ref[0:tall, :].astype(BF16)

    def forward(k):
        scratch[4 * k + 1][...] = dot_nn(wws_ref[...], xa_ref[0:rows, cols[k]])

    def logits(k):
        x_ref, pre_ref, act_ref, slope_ref = scratch[4 * k : 4 * k + 4]
        total = jnp.zeros((8, width), F32)
        for a, b in cuts:
            cp = pre_ref[hidden + a : hidden + b, :] + wide(cb_ref[a:b, :], width)
            pre_ref[hidden + a : hidden + b, :] = cp
            term = (x_ref[a:b, :] * cp) * wide(hc_ref[a:b, :], width)
            for r in range(0, b - a, 8):
                total = total + term[r : r + 8]
        for a, b in hid_cuts:
            v = pre_ref[a:b, :] + wide(db_ref[a:b, :], width)
            vv = v * v
            half = 0.5 + 0.5 * jnp.tanh(v * (GELU_S + (GELU_S * GELU_C) * vv))
            act = v * half
            act_ref[a:b, :] = act
            slope_ref[a:b, :] = half + (act * (1.0 - half)) * ((2.0 * GELU_S) + (6.0 * GELU_S * GELU_C) * vv)
            term = act * wide(hd_ref[a:b, :], width)
            for r in range(0, b - a, 8):
                total = total + term[r : r + 8]
        logit = jnp.sum(total, axis=0, keepdims=True) + hb_ref[0:1, 0:1]
        logit_ref[:, cols[k]] = logit
        labels = lab_ref[:, cols[k]].astype(F32)
        small = jnp.exp(-jnp.abs(logit))
        loss = jnp.maximum(logit, 0.0) + jnp.log1p(small) - labels * logit
        sig = jnp.where(logit >= 0.0, 1.0, small) / (1.0 + small)
        dlogit = (sig - labels) * scale
        sc_ref[0:1, :] += fold(loss)
        sc_ref[1:2, :] += fold(dlogit)
        top_ref[...] = jnp.maximum(top_ref[...], jnp.abs(dlogit))
        return dlogit

    def gradients(k, dlogit):
        x_ref, pre_ref, act_ref, slope_ref = scratch[4 * k : 4 * k + 4]
        for a, b in hid_cuts:
            hda_ref[a:b, :] += fold(dlogit * act_ref[a:b, :])
            dd = (dlogit * wide(hd_ref[a:b, :], width)) * slope_ref[a:b, :]
            grad_ref[a:b, cols[k]] = dd.astype(BF16)
        for a, b in cuts:
            cp = pre_ref[hidden + a : hidden + b, :]
            dx = dlogit * x_ref[a:b, :]
            hc = wide(hc_ref[a:b, :], width)
            hca_ref[a:b, :] += fold(dx * cp)
            dc = dx * hc
            if b == rows:
                dc = jnp.concatenate([dc, jnp.zeros((tall - rows, width), F32)], axis=0)
            grad_ref[hidden + a : hidden + a + dc.shape[0], cols[k]] = dc.astype(BF16)
            pre_ref[hidden + a : hidden + b, :] = (dlogit * hc) * cp

    def backward(k):
        x_ref, pre_ref = scratch[4 * k], scratch[4 * k + 1]
        x_ref[0:rows, :] = pre_ref[hidden:, :] + dot_nn(wbs_ref[...], grad_ref[0 : hidden + rows, cols[k]])

    def give(k):
        x_ref = scratch[4 * k]
        for f in range(fields):
            demb_ref[f, :, cols[k]] = x_ref[emb * f : emb * f + PAD, :].astype(BF16)
        dg_ref[:, cols[k]] = x_ref[cat:full, :] * dm_ref[:, cols[k]].astype(F32)

    dlogits = {}
    for phase, k in ORDER[tiles]:
        if phase == "w":
            pl.when(start)(loads[k].wait)
        elif phase == "x":
            gather(k)
        elif phase == "f":
            forward(k)
        elif phase == "l":
            dlogits[k] = logits(k)
        elif phase == "g":
            gradients(k, dlogits[k])
        elif phase == "b":
            backward(k)
        else:
            give(k)

    @pl.when(pl.program_id(0) == pl.num_programs(0) - 1)
    def _():
        each = jnp.zeros((8, 128), F32)
        for ref in (hca_ref, hda_ref, sc_ref):
            each = peak(each, ref[...])
        heads = jnp.zeros((8, 128), F32)
        for ref, most in ((hc_ref, X_TOP), (hd_ref, SLOPE_TOP)):
            heads = jnp.maximum(heads, most * peak(jnp.zeros((8, 128), F32), ref[...]))
        products = jnp.max(jnp.max(heads, axis=1, keepdims=True), axis=0, keepdims=True) * (
            X_TOP * tiles * TILE * pl.num_programs(0)
        )
        products = products * jnp.maximum(top_ref[:, 0:128], top_ref[:, 128:256])
        expo_ref[...] = exponents(jnp.maximum(each * 128.0, products))


ORDER = {
    2: [
        ("x", 0), ("x", 1), ("w", 0), ("f", 0), ("f", 1), ("l", 0), ("w", 1), ("l", 1),
        ("g", 0), ("b", 0), ("g", 1), ("b", 1), ("o", 0), ("o", 1),
    ],
}


TILES = 2


def layers(chunks, dense_values, dense_present, labels, weights, columns, emb, scale):
    fields = sum(c.shape[0] for c in chunks)
    dense, examples = dense_values.shape
    hidden = columns[1].shape[0]
    rows = columns[0].shape[0]
    tall = ceil_to(rows, 16)
    take = TILES * TILE
    column = lambda r: pl.BlockSpec((r, take), lambda t: (0, t))
    whole = lambda a: pl.BlockSpec(a.shape, lambda t: (0,) * a.ndim, pipeline_mode=pl.Buffered(1))
    kept = lambda r: pl.BlockSpec((r, 128), lambda t: (0, 0))
    shape = jax.ShapeDtypeStruct
    return pl.pallas_call(
        lambda *refs: layers_kernel((fields, emb, dense, len(chunks), TILES), scale, *refs),
        grid=(examples // take,),
        in_specs=[pl.BlockSpec((c.shape[0], PAD, take), lambda t: (0, 0, t)) for c in chunks]
        + [column(dense), column(dense), column(1)]
        + [pl.BlockSpec(memory_space=pltpu.HBM) for _ in weights]
        + [whole(a) for a in columns],
        out_specs=[
            column(1),
            column(tall),
            column(hidden + tall),
            pl.BlockSpec((fields, PAD, take), lambda t: (0, 0, t)),
            column(dense),
            kept(rows),
            kept(hidden),
            kept(8),
            kept(8),
        ],
        out_shape=[
            shape((1, examples), F32),
            shape((tall, examples), BF16),
            shape((hidden + tall, examples), BF16),
            shape((fields, PAD, examples), BF16),
            shape((dense, examples), F32),
            shape((rows, 128), F32),
            shape((hidden, 128), F32),
            shape((8, 128), F32),
            shape((8, 128), F32),
        ],
        scratch_shapes=[pltpu.VMEM((8, TILE), F32)]
        + [pltpu.VMEM(w.shape, BF16) for w in weights]
        + [pltpu.SemaphoreType.DMA((2,))]
        + [
            pltpu.VMEM((tall, TILE), F32),
            pltpu.VMEM((rows + hidden, TILE), F32),
            pltpu.VMEM((hidden, TILE), F32),
            pltpu.VMEM((hidden, TILE), F32),
        ]
        * TILES,
        compiler_params=params(40),
        cost_estimate=cost(2 * examples * rows * (2 * rows + 2 * hidden), 9 * 2**20 + 20 * rows * examples),
        name="layers",
    )(*chunks, dense_values, dense_present, labels, *map(in_hbm, weights), *columns)


def weight_kernel(rows, examples_all, half_ref, *refs):
    xa_ref, dd_ref, dc_ref, dct_ref, hc_ref, hct_ref, hd_ref, sc_ref, expo_ref, out_ref, over = refs
    quarter = out_ref.shape[2] - FRONT
    half, j = half_ref[0], pl.program_id(0)
    first = half * pl.num_programs(0) + j == 0
    x = xa_ref[0:rows, :]
    hidden = over.shape[1] - 128

    @pl.when(j == 0)
    def _():
        tail = dot_nt(x, dct_ref[...])
        tail = jnp.concatenate([tail, jnp.zeros((rows, 128 - 16), F32)], axis=1)
        for r in range(0, hidden, 128):
            over[:, r : r + 128] = tail[r : r + 128].T[0:8]
        last = jnp.concatenate([tail[hidden:rows], jnp.zeros((128 - rows + hidden, 128), F32)], axis=0)
        over[:, hidden:] = last.T[0:8]

    deep = dot_nt(x, dd_ref[...])
    cross = dot_nt(x, dc_ref[...])
    at = pl.multiple_of((half * pl.num_programs(0) + j) * TILE, TILE)
    total = lambda ref: jnp.sum(ref[...].T, axis=0, keepdims=True)
    row = lax.broadcasted_iota(jnp.int32, (8, TILE), 0)
    heads = jnp.where(row == 0, total(hc_ref), jnp.where(row == 1, total(hd_ref), 0.0))
    zeros = lambda n, m: jnp.zeros((n, m), F32)
    corner = jnp.concatenate([over[0:3, hidden:], zeros(3, TILE - 128)], axis=1)
    small = jnp.concatenate([zeros(2, TILE), corner, zeros(3, TILE)], axis=0)
    ends = jnp.concatenate([hct_ref[...], zeros(120, 128)], axis=0)
    ends = jnp.concatenate([total(ends), zeros(1, TILE - 128)], axis=1)
    sums = jnp.sum(sc_ref[...], axis=1, keepdims=True)
    lane = lax.broadcasted_iota(jnp.int32, (8, TILE), 1)
    scalars = jnp.where(lane == 0, sums[0:1] / examples_all, jnp.where(lane == 1, sums[1:2], 0.0))
    small = small + jnp.where(row == 5, ends, 0.0) + jnp.where(row == 6, scalars, 0.0)
    heads = heads + jnp.where(first, small, 0.0)
    parts = [(0, deep), (rows, cross), (2 * rows, over[:, pl.ds(at, TILE)]), (2 * rows + 8, heads)]
    for q in range(4):
        for h in range(2):
            out_ref[q, h, 0:FRONT, :] = expo_ref[...]
    for base, part in parts:
        at = 0
        while at < part.shape[0]:
            q, r = divmod(base + at, quarter)
            n = min(part.shape[0] - at, quarter - r)
            place = jnp.where(half == 0, (0, 2, 1, 3)[q], q)
            for h in range(2):
                out_ref[place, h, FRONT + r : FRONT + r + n, :] = part[at : at + n, h * 128 : (h + 1) * 128]
            at += n


def weight_grads(half, xa, grads, hca, hda, sc, expo, examples_all):
    tall, examples = xa.shape
    rows, hidden = hca.shape[0], hda.shape[0]
    quarter = ceil_to(2 * rows + 16, 32) // 4
    steps = hidden // TILE // 2
    return pl.pallas_call(
        lambda *refs: weight_kernel(rows, examples_all, *refs),
        grid_spec=pltpu.PrefetchScalarGridSpec(
            num_scalar_prefetch=1,
            grid=(steps,),
            in_specs=[
                pl.BlockSpec((tall, examples), lambda j, h: (0, 0), pipeline_mode=pl.Buffered(1)),
                pl.BlockSpec((TILE, examples), lambda j, h: (h[0] * steps + j, 0)),
                pl.BlockSpec((TILE, examples), lambda j, h: (2 * steps + h[0] * steps + j, 0)),
                pl.BlockSpec((16, examples), lambda j, h: (2 * hidden // 16, 0)),
                pl.BlockSpec((TILE, 128), lambda j, h: (h[0] * steps + j, 0)),
                pl.BlockSpec((8, 128), lambda j, h: (hidden // 8, 0)),
                pl.BlockSpec((TILE, 128), lambda j, h: (h[0] * steps + j, 0)),
                pl.BlockSpec((8, 128), lambda j, h: (0, 0)),
                pl.BlockSpec((8, 128), lambda j, h: (0, 0)),
            ],
            out_specs=pl.BlockSpec((4, 2, FRONT + quarter, 128), lambda j, h: (0, j, 0, 0)),
            scratch_shapes=[pltpu.VMEM((8, hidden + 128), F32)],
        ),
        out_shape=jax.ShapeDtypeStruct((4, 2 * steps, FRONT + quarter, 128), F32),
        compiler_params=params(16),
        cost_estimate=cost(2 * examples * rows * hidden, 10 * rows * hidden),
        name="weight_grads",
    )(half.reshape(1).astype(jnp.int32), xa, *[in_hbm(grads)] * 3, *map(in_hbm, (hca, hca, hda)), sc, expo)


def spread_kernel(first, core_ref, place_ref, block_ref, own_ref, sib_ref, out_ref, expo_ref, top_ref):
    count, _, examples = own_ref.shape
    n_blocks = out_ref.shape[0] * out_ref.shape[1]

    @pl.when(pl.program_id(0) == 0)
    def _():
        top_ref[...] = jnp.zeros_like(top_ref)

    core = core_ref[0]
    every = []
    for k in range(count):
        f = first + pl.program_id(0) * count + k
        sums = jnp.zeros((n_blocks * PAD, HI), F32)
        for s, ref in enumerate((own_ref, sib_ref)):
            base = (core if s == 0 else 1 - core) * examples
            for at in range(0, examples, WIDE):
                cols = pl.ds(pl.multiple_of(base + at, WIDE), WIDE)
                place = place_ref[pl.ds(f, 1), cols]
                block = block_ref[pl.ds(f, 1), cols]
                grads = ref[k, :, at : at + WIDE].astype(F32)
                chosen = [jnp.where(block == b, grads, 0.0) for b in range(n_blocks)]
                chosen = jnp.concatenate(chosen, axis=0).astype(BF16)
                sums = sums + dot_nt(chosen, onehot_rows(place, WIDE))
        every.append(sums)
    for k, sums in enumerate(every):
        top_ref[...] = peak(top_ref[...], sums)
        for b in range(n_blocks):
            for h in range(2):
                out_ref[b // out_ref.shape[1], b % out_ref.shape[1], h, k * PAD : (k + 1) * PAD] = sums[
                    b * PAD : (b + 1) * PAD, h * 128 : (h + 1) * 128
                ]

    @pl.when(pl.program_id(0) == pl.num_programs(0) - 1)
    def _():
        expo_ref[...] = exponents(jnp.maximum(top_ref[:, 0:128], top_ref[:, 128:256]))


def spread(core, place, block, own, sib, first, count, blocks):
    fields, _, examples = own.shape
    whole = lambda a: pl.BlockSpec(a.shape, lambda f: (0, 0), pipeline_mode=pl.Buffered(1))
    take = 2
    return pl.pallas_call(
        lambda *refs: spread_kernel(first, *refs),
        grid=(count // take,),
        in_specs=[pl.BlockSpec(memory_space=pltpu.SMEM), whole(place), whole(block)]
        + [pl.BlockSpec((take, PAD, examples), lambda f: (f + first // take, 0, 0))] * 2,
        out_specs=[
            pl.BlockSpec((2, blocks, 2, take * PAD, 128), lambda f: (0, 0, 0, f, 0)),
            pl.BlockSpec((8, 128), lambda f: (0, 0)),
        ],
        out_shape=[
            jax.ShapeDtypeStruct((2, blocks, 2, count * PAD, 128), F32),
            jax.ShapeDtypeStruct((8, 128), F32),
        ],
        scratch_shapes=[pltpu.VMEM((8, HI), F32)],
        compiler_params=params(10),
        cost_estimate=cost(8 * count * blocks * PAD * HI * examples, 4 * count * PAD * 16 * 128 * blocks),
        name="spread",
    )(core.reshape(1).astype(jnp.int32), place, block, own, sib)


def flip(array, axis, bit):
    size = lax.axis_size(axis)
    return lax.ppermute(array, axis, [(i, i ^ (1 << bit)) for i in range(size)])


def bit_of(axis, bit):
    return (lax.axis_index(axis) >> bit) & 1


def crossed_pairs(stage, n_dp, n_mp):
    pairs = []
    for d in range(n_dp):
        for m in range(n_mp):
            along_dp = (m & 1) == stage
            to = (d ^ 1, m) if along_dp else (d, m ^ 2)
            pairs.append((d * n_mp + m, to[0] * n_mp + to[1]))
    return pairs


def crossed_flip(array, stage):
    return lax.ppermute(array, ("dp", "mp"), crossed_pairs(stage, lax.axis_size("dp"), lax.axis_size("mp")))


def crossed_bit(stage):
    return jnp.where(bit_of("mp", 0) == stage, bit_of("dp", 0), bit_of("mp", 1))


def after(value, token):
    return lax.optimization_barrier((value, token))[0]


def encode(values, expo, at):
    row = lax.broadcasted_iota(jnp.int32, values.shape, values.ndim - 2)
    here = expo.reshape((1,) * (values.ndim - 1) + (128,))
    return jnp.where(row == at, here, values * jnp.exp2(-here)).astype(F16)


def add(kept, expo, got, at):
    theirs = got[(0,) * (got.ndim - 2) + (at,)].astype(F32)
    total = kept + got.astype(F32) * jnp.exp2(theirs).reshape((1,) * (got.ndim - 1) + (128,))
    return total, jnp.maximum(expo, theirs) + 1.0


def reduction(acc, expo, at, z_dim):
    for k, (mine, send) in enumerate(stages()):
        if k == 2:
            acc = jnp.swapaxes(acc.reshape(2, 2, *acc.shape[z_dim:]), 0, 1)
        away = lax.dynamic_index_in_dim(acc, 1 - mine, 0, keepdims=False)
        kept = lax.dynamic_index_in_dim(acc, mine, 0, keepdims=False)
        message = encode(away, expo, at)
        got = send(message)
        token = yield message
        acc, expo = add(kept, expo, after(got, token), at)
    yield acc, expo


def gathering(piece, core):
    for mine, send in [*reversed(stages()), (core, lambda a: flip(a, "mp", 0))]:
        other = send(piece)
        token = yield piece
        other = after(other, token)
        low = mine == 0
        piece = jnp.stack([jnp.where(low, piece, other), jnp.where(low, other, piece)], axis=0)
    yield piece


def stages():
    return [
        (crossed_bit(0), lambda a: crossed_flip(a, 0)),
        (crossed_bit(1), lambda a: crossed_flip(a, 1)),
        (bit_of("dp", 1), lambda a: flip(a, "dp", 1)),
        (bit_of("dp", 2), lambda a: flip(a, "dp", 2)),
    ]


def assemble_kernel(rows, full, in_ref, over_ref, cross_ref, deep_ref, vec_ref):
    t = pl.program_id(0)
    last = pl.num_programs(0) - 1

    @pl.when(t < last)
    def _():
        for h in range(2):
            cols = slice(h * 128, (h + 1) * 128)
            parts = []
            for q in range(4):
                ahead = jnp.where(t < last // 2, q % 2, q // 2)
                parts.append(in_ref[0, ahead, q // 2 + q % 2 - ahead, h, 0, FRONT:, :])
            every = jnp.concatenate(parts, axis=0)
            deep_ref[:, cols] = every[0:full]
            cross_ref[:, cols] = every[rows : rows + full]
            vec_ref[0:1, cols] = every[rows + full : rows + full + 1]
            vec_ref[1:2, cols] = every[full : full + 1]
            vec_ref[2:4, cols] = every[2 * rows + 8 : 2 * rows + 10]
            vec_ref[4:8, cols] = every[2 * rows + 12 : 2 * rows + 16]

    @pl.when(t == last)
    def _():
        cross_ref[:, 0:128] = over_ref[0:full, :]


def assemble(pieces, rows, full, hidden):
    steps = hidden // 256
    quarter = pieces.shape[5] - FRONT
    half = steps // 2
    spare = pieces[:, 1, 1, :, :, FRONT + quarter - 16 :, :].transpose(3, 0, 2, 1, 4).reshape(16, hidden)
    extra = full - hidden
    over = jnp.concatenate([spare[0:extra], spare[10 : 10 + extra, 0 : rows - hidden]], axis=1)
    over = jnp.pad(over.T, ((0, 0), (0, 128 - extra)))
    now = lambda t: jnp.minimum(t, steps - 1)
    return pl.pallas_call(
        lambda *refs: assemble_kernel(rows, full, *refs),
        grid=(steps + 1,),
        in_specs=[
            pl.BlockSpec(
                (1, 2, 2, 2, 1, FRONT + quarter, 128), lambda t: (now(t) // half, 0, 0, 0, now(t) % half, 0, 0)
            ),
            pl.BlockSpec((rows, 128), lambda t: (0, 0)),
        ],
        out_specs=[
            pl.BlockSpec((full, 256), lambda t: (0, t)),
            pl.BlockSpec((full, 256), lambda t: (0, now(t))),
            pl.BlockSpec((8, 256), lambda t: (0, now(t))),
        ],
        out_shape=[
            jax.ShapeDtypeStruct((full, full), F32),
            jax.ShapeDtypeStruct((full, hidden), F32),
            jax.ShapeDtypeStruct((8, hidden), F32),
        ],
        compiler_params=params(10),
        cost_estimate=cost(0, 16 * rows * hidden),
        name="assemble",
    )(pieces, over), over


def table_place(ids, table_rows, n_dp, core):
    upper = ids // (2 * table_rows)
    rest = ids % table_rows
    if n_dp == 8:
        piece = table_rows // n_dp
        at = rest // piece
        low = at % 2
        first = jnp.where(core == 0, low, upper)
        second = jnp.where(core == 0, upper, low)
        block = first * 4 + second * 2 + at // 4
        place = (at // 2) % 2 * piece + rest % piece
    else:
        block = upper * (table_rows // HI) + rest // HI
        place = rest % HI
    return place, jnp.where((ids // table_rows) % 2 == core, block, -1)


def body(
    field_ids,
    field_present,
    dense_values,
    dense_present,
    clicked,
    tables,
    cross_weight,
    cross_bias,
    deep_weight,
    deep_bias,
    head_cross,
    head_deep,
    head_bias,
):
    fields, batch_group = field_ids.shape
    table_rows, cat = tables.shape
    emb = cat // fields
    full, hidden = deep_weight.shape
    dense = full - cat
    n_dp, n_mp = lax.axis_size("dp"), lax.axis_size("mp")
    examples = batch_group // n_mp
    examples_all = batch_group * n_dp
    blocks = table_rows // HI
    rows = ceil_to(full + 1, 8)
    me = lax.axis_index("mp")
    core = me & 1

    chosen = jnp.where(field_present > 0, field_ids, 0)
    own_ids = lax.dynamic_slice_in_dim(chosen, me * examples, examples, 1)
    place_own = own_ids & (HI - 1)
    block_own = (own_ids // HI) ^ (me * blocks)
    pair_ids = lax.dynamic_slice_in_dim(chosen, (me - core) * examples, 2 * examples, 1)
    place, block = table_place(pair_ids, table_rows, n_dp, core)

    columns = tables.T
    cuts = [(0, 11), (11, 22), (22, fields)]
    far = [flip(columns[a * emb : b * emb], "mp", 1) for a, b in cuts]
    near = flip(columns, "mp", 0)
    weights = prepare(cross_weight, deep_weight, cross_bias, deep_bias, head_cross, head_deep, rows)
    token = weights[0]
    found = []
    for k, (a, b) in enumerate(cuts):
        far_near = flip(after(far[k], token), "mp", 0)
        found.append(lookup(place_own[a:b], block_own[a:b], (columns, near, far[k], far_near), a * emb, emb))
        token = found[-1]

    logit, xa, grads, demb, dense_grad, hca, hda, sc, expo = layers(
        found,
        dense_values,
        dense_present,
        clicked[None, :],
        weights[:2],
        (*weights[2:], jnp.broadcast_to(head_bias[:, None], (8, 128))),
        emb,
        1.0 / math.sqrt(examples_all),
    )
    demb_sib = flip(demb, "mp", 0)
    grad_args = (xa, grads, hca, hda, sc, expo, examples_all)
    away = weight_grads(1 - core, *grad_args)
    if n_dp == 8:
        away = encode(away, expo[0], FRONT - 1)
    got = flip(away, "mp", 0)
    sums = weight_grads(after(core, away), *grad_args)
    halves = [(0, 12), (12, fields)]

    def table_part(token, k):
        a, b = halves[k]
        part, top = spread(core, place, block, after(demb, token), demb_sib, a, b - a, blocks)
        return part, top[0]

    if n_dp == 8:
        got = after(got, sums)
        both, expo = add(sums, expo[0], got, FRONT - 1)
        both = both.reshape(2, 2, *sums.shape[1:])
        weight_chain = reduction(both, expo, FRONT - 1, 1)
        token = next(weight_chain)
        table_chains = []
        for k in range(2):
            part, top = table_part(token, k)
            part = part.reshape(2, 2, 2, 2, *part.shape[3:])
            table_chains.append(reduction(part, top, PAD - 1, 2))
            token = next(table_chains[k])
            token = weight_chain.send(token)
        token = table_chains[0].send(token)
        token = weight_chain.send(token)
        token = table_chains[1].send(token)
        token = table_chains[0].send(token)
        total, expo = weight_chain.send(token)
        total = (total * jnp.exp2(-expo)[None, :]).astype(F16)
        weight_chain = gathering(total, core)
        token = next(weight_chain)
        token = table_chains[1].send(token)
        token = table_chains[0].send(token)
        token = weight_chain.send(token)
        token = table_chains[1].send(token)
        token = weight_chain.send(token)
        first_part, _ = table_chains[0].send(token)
        token = weight_chain.send(first_part)
        second_part, _ = table_chains[1].send(token)
        token = weight_chain.send(second_part)
        pieces = weight_chain.send(token)
        pieces = pieces.astype(F32) * jnp.exp2(expo)
        table_out = jnp.concatenate([first_part, second_part], axis=0)
    else:
        summed = lax.psum(sums + got, "dp")
        summed = summed + flip(summed, "mp", 1)
        pieces = lax.all_gather(summed, "mp")[0:2].reshape(2, 2, 2, 2, 2, *sums.shape[2:])
        pieces = jnp.swapaxes(pieces, 3, 4)
        table_out = jnp.concatenate([table_part(sums, k)[0] for k in range(2)], axis=3)
        table_out = table_out.transpose(0, 3, 1, 2, 4).reshape(2, fields * PAD, table_rows)
        upper = bit_of("mp", 1)
        away = lax.dynamic_index_in_dim(table_out, 1 - upper, 0, keepdims=False)
        table_out = lax.dynamic_index_in_dim(table_out, upper, 0, keepdims=False) + flip(away, "mp", 1)
        table_out = lax.psum_scatter(table_out, "dp", scatter_dimension=1, tiled=True)
    tables_grad = table_out.reshape(fields, PAD, -1)[:, :emb].reshape(cat, -1).T
    (cross_grad, deep_grad, small), over = assemble(pieces, rows, full, hidden)
    return (
        logit[0],
        small[6, 0],
        dense_grad,
        tables_grad,
        cross_grad,
        jnp.concatenate([small[0], over[full, 0 : full - hidden]]),
        deep_grad,
        small[1],
        jnp.concatenate([small[2], small[5, 0 : full - hidden]]),
        small[3],
        small[6, 1:2],
    )


def solution(mesh):
    placed = (
        P(None, "dp"),
        P(None, "dp"),
        P(None, ("dp", "mp")),
        P(None, ("dp", "mp")),
        P(("dp", "mp")),
        P("mp", None),
        P(),
        P(),
        P(),
        P(),
        P(),
        P(),
        P(),
    )
    return jax.shard_map(
        body,
        mesh=mesh,
        in_specs=placed,
        out_specs=(
            P(("dp", "mp")),
            P(),
            P(None, ("dp", "mp")),
            P(("mp", "dp"), None),
            P(),
            P(),
            P(),
            P(),
            P(),
            P(),
            P(),
        ),
        check_vma=False,
    )
```

```python
import math

import jax
import jax.numpy as jnp
from jax import lax
from jax.experimental import pallas as pl
from jax.experimental.pallas import tpu as pltpu
from jax.sharding import PartitionSpec as P

BF16, F32, F16 = jnp.bfloat16, jnp.float32, jnp.float16
HI = 256
SLOPE_TOP = 1.25
X_TOP = 6.0
FRONT = 8
PAD = 40
TILE = 256
CUTS = (13, 22)
WIDE = 512
GELU_S = math.sqrt(2.0 / math.pi)
GELU_C = 0.044715


def params(mebibytes):
    return pltpu.CompilerParams(vmem_limit_bytes=mebibytes * 1024 * 1024)


def cost(flops, moved):
    return pl.CostEstimate(flops=int(flops), bytes_accessed=int(moved), transcendentals=0)


def in_hbm(array):
    return pltpu.with_memory_space_constraint(array, pltpu.HBM)


def in_vmem(array):
    return pltpu.with_memory_space_constraint(array, pltpu.VMEM)


def ceil_to(value, unit):
    return -(-value // unit) * unit


def dot_nn(left, right):
    return jnp.dot(left, right, preferred_element_type=F32)


def dot_nt(left, right, precision=None):
    return lax.dot_general(
        left, right, (((1,), (1,)), ((), ())), preferred_element_type=F32, precision=precision
    )


def onehot_rows(place, width):
    rows = lax.broadcasted_iota(jnp.int16, (HI, width), 0)
    return jnp.where(rows == place.astype(jnp.int16), jnp.ones((), BF16), jnp.zeros((), BF16))


def prepare_kernel(cw_ref, dw_ref, cb_ref, db_ref, hc_ref, hd_ref, ww_ref, wb_ref, cbo_ref, dbo_ref, hco_ref, hdo_ref, pad):
    full, hidden = dw_ref.shape
    rows = wb_ref.shape[0]
    pad[...] = jnp.zeros_like(pad)
    for source, base, width in ((dw_ref, 0, hidden), (cw_ref, hidden, full)):
        pad[0:full, 0:width] = source[...].astype(F32)
        if width < rows:
            pad[:, width:] = jnp.zeros((pad.shape[0], pad.shape[1] - width), F32)
        wide_width = hidden if base == 0 else rows
        wb_ref[:, base : base + wide_width] = pad[0:rows, 0:wide_width].astype(BF16)
        for r in range(0, wide_width, 128):
            n = min(128, wide_width - r)
            turned = pad[:, r : r + 128].T
            ww_ref[base + r : base + r + n, :] = turned[0:n, 0:rows].astype(BF16)
    for source, out, more in ((cb_ref, cbo_ref, 1.0), (db_ref, dbo_ref, 0.0), (hc_ref, hco_ref, 0.0), (hd_ref, hdo_ref, 0.0)):
        for r in range(0, out.shape[0], 128):
            n = min(128, out.shape[0] - r)
            line = source[:, r : r + 128]
            out[r : r + n, :] = (jnp.broadcast_to(line, (128, 128)).T + more)[0:n]


def prepare(cross_weight, deep_weight, cross_bias, deep_bias, head_cross, head_deep, rows):
    full, hidden = deep_weight.shape
    wide_rows = ceil_to(rows, 128)
    line = lambda v: jnp.pad(v, (0, ceil_to(v.shape[0], 128) - v.shape[0]))[None, :]
    shape = jax.ShapeDtypeStruct
    return pl.pallas_call(
        prepare_kernel,
        out_shape=[
            shape((hidden + rows, rows), BF16),
            shape((rows, hidden + rows), BF16),
            shape((rows, 128), F32),
            shape((hidden, 128), F32),
            shape((rows, 128), F32),
            shape((hidden, 128), F32),
        ],
        scratch_shapes=[pltpu.VMEM((wide_rows, wide_rows), F32)],
        compiler_params=params(16),
        cost_estimate=cost(0, 16 * rows * rows),
        name="prepare",
    )(cross_weight, deep_weight, line(cross_bias), line(deep_bias), line(head_cross), line(head_deep))


def lookup_kernel(emb, blocks, at_row, place_ref, block_ref, *refs):
    sources, out_ref, flat, packed = refs[0:4], refs[4], refs[5], refs[6]
    n_fields, examples = place_ref.shape
    rows = emb * n_fields
    for s, source in enumerate(sources):
        first = at_row if s < 2 else 0
        flat[s, 0:rows, :] = source[first : first + rows, :].astype(F32)
    for f in range(n_fields):
        for s in range(4):
            for b in range(blocks):
                piece = flat[s, emb * f : emb * f + PAD, b * HI : (b + 1) * HI]
                at = (s * blocks + b) * PAD
                packed[f, at : at + PAD, :] = piece.astype(BF16)

    for f in range(n_fields):
        block = block_ref[f : f + 1, :]
        found = dot_nn(packed[f], onehot_rows(place_ref[f : f + 1, :], examples))
        acc = found[0:PAD]
        for b in range(1, 4 * blocks):
            acc = jnp.where(block == b, found[b * PAD : (b + 1) * PAD], acc)
        out_ref[f] = acc.astype(BF16)


def lookup(place, block, sources, at_row, emb):
    n_fields, examples = place.shape
    width = sources[0].shape[1]
    blocks = width // HI
    n_rows = 4 * blocks * PAD
    return pl.pallas_call(
        lambda *refs: lookup_kernel(emb, blocks, at_row, *refs),
        out_shape=jax.ShapeDtypeStruct((n_fields, PAD, examples), BF16),
        scratch_shapes=[
            pltpu.VMEM((4, ceil_to(n_fields * emb, 8) + 8, width), F32),
            pltpu.VMEM((n_fields, n_rows, HI), BF16),
        ],
        compiler_params=params(16),
        cost_estimate=cost(2 * n_fields * n_rows * HI * examples, 4 * n_fields * PAD * examples),
        name="lookup",
    )(place, block, *sources)


def wide(column, width):
    return jnp.concatenate([column] * (width // 128), axis=1)


def fold(values):
    total = values[:, 0:128]
    for at in range(128, values.shape[1], 128):
        total = total + values[:, at : at + 128]
    return total


def peak(top, values):
    for r in range(0, values.shape[0], 8):
        top = jnp.maximum(top, jnp.abs(values[r : r + 8]))
    return top


def exponents(top):
    most = jnp.max(jnp.max(top, axis=1, keepdims=True), axis=0, keepdims=True)
    return jnp.broadcast_to(jnp.ceil(jnp.log(jnp.maximum(most, 1e-30)) * (1.0 / math.log(2.0))) - 14.0, (8, 128))


def layers_kernel(sizes, scale, *refs):
    fields, emb, dense, n_chunks, tiles = sizes
    chunks = refs[:n_chunks]
    (dv_ref, dm_ref, lab_ref, ww_ref, wb_ref, cb_ref, db_ref, hc_ref, hd_ref, hb_ref) = refs[n_chunks : n_chunks + 10]
    (logit_ref, xa_ref, grad_ref, demb_ref, dg_ref, hca_ref, hda_ref, sc_ref, expo_ref) = refs[
        n_chunks + 10 : n_chunks + 19
    ]
    top_ref, wws_ref, wbs_ref, sems, *scratch = refs[n_chunks + 19 :]
    loads = [
        pltpu.make_async_copy(ww_ref, wws_ref, sems.at[0]),
        pltpu.make_async_copy(wb_ref, wbs_ref, sems.at[1]),
    ]
    start = pl.program_id(0) == 0
    hidden = hda_ref.shape[0]
    rows = hca_ref.shape[0]
    width = TILE
    cat = fields * emb
    full = cat + dense
    step = 128
    cuts = [(a, min(a + step, rows)) for a in range(0, rows, step)]
    hid_cuts = [(a, min(a + step, hidden)) for a in range(0, hidden, step)]
    cols = [slice(k * TILE, (k + 1) * TILE) for k in range(tiles)]
    tall = xa_ref.shape[0]

    @pl.when(start)
    def _():
        for load in loads:
            load.start()
        hca_ref[...] = jnp.zeros_like(hca_ref)
        hda_ref[...] = jnp.zeros_like(hda_ref)
        sc_ref[...] = jnp.zeros_like(sc_ref)
        top_ref[...] = jnp.zeros_like(top_ref)

    def gather(k):
        x_ref = scratch[4 * k]
        f = 0
        for chunk in chunks:
            for c in range(chunk.shape[0]):
                x_ref[emb * f : emb * f + PAD, :] = chunk[c, :, cols[k]].astype(F32)
                f += 1
        x_ref[cat:full, :] = dv_ref[:, cols[k]] * dm_ref[:, cols[k]].astype(F32)
        x_ref[full:tall, :] = (
            lax.broadcasted_iota(jnp.int32, (tall - full, width), 0) == 0
        ).astype(F32)
        xa_ref[:, cols[k]] = x_ref[0:tall, :].astype(BF16)

    def forward(k):
        scratch[4 * k + 1][...] = dot_nn(wws_ref[...], xa_ref[0:rows, cols[k]])

    def logits(k):
        x_ref, pre_ref, act_ref, slope_ref = scratch[4 * k : 4 * k + 4]
        total = jnp.zeros((8, width), F32)
        for a, b in cuts:
            cp = pre_ref[hidden + a : hidden + b, :] + wide(cb_ref[a:b, :], width)
            pre_ref[hidden + a : hidden + b, :] = cp
            term = (x_ref[a:b, :] * cp) * wide(hc_ref[a:b, :], width)
            for r in range(0, b - a, 8):
                total = total + term[r : r + 8]
        for a, b in hid_cuts:
            v = pre_ref[a:b, :] + wide(db_ref[a:b, :], width)
            vv = v * v
            half = 0.5 + 0.5 * jnp.tanh(v * (GELU_S + (GELU_S * GELU_C) * vv))
            act = v * half
            act_ref[a:b, :] = act
            slope_ref[a:b, :] = half + (act * (1.0 - half)) * ((2.0 * GELU_S) + (6.0 * GELU_S * GELU_C) * vv)
            term = act * wide(hd_ref[a:b, :], width)
            for r in range(0, b - a, 8):
                total = total + term[r : r + 8]
        logit = jnp.sum(total, axis=0, keepdims=True) + hb_ref[0:1, 0:1]
        logit_ref[:, cols[k]] = logit
        labels = lab_ref[:, cols[k]].astype(F32)
        small = jnp.exp(-jnp.abs(logit))
        loss = jnp.maximum(logit, 0.0) + jnp.log1p(small) - labels * logit
        sig = jnp.where(logit >= 0.0, 1.0, small) / (1.0 + small)
        dlogit = (sig - labels) * scale
        sc_ref[0:1, :] += fold(loss)
        sc_ref[1:2, :] += fold(dlogit)
        top_ref[...] = jnp.maximum(top_ref[...], jnp.abs(dlogit))
        return dlogit

    def gradients(k, dlogit):
        x_ref, pre_ref, act_ref, slope_ref = scratch[4 * k : 4 * k + 4]
        for a, b in hid_cuts:
            hda_ref[a:b, :] += fold(dlogit * act_ref[a:b, :])
            dd = (dlogit * wide(hd_ref[a:b, :], width)) * slope_ref[a:b, :]
            grad_ref[a:b, cols[k]] = dd.astype(BF16)
        for a, b in cuts:
            cp = pre_ref[hidden + a : hidden + b, :]
            dx = dlogit * x_ref[a:b, :]
            hc = wide(hc_ref[a:b, :], width)
            hca_ref[a:b, :] += fold(dx * cp)
            dc = dx * hc
            if b == rows:
                dc = jnp.concatenate([dc, jnp.zeros((tall - rows, width), F32)], axis=0)
            grad_ref[hidden + a : hidden + a + dc.shape[0], cols[k]] = dc.astype(BF16)
            pre_ref[hidden + a : hidden + b, :] = (dlogit * hc) * cp

    def backward(k):
        x_ref, pre_ref = scratch[4 * k], scratch[4 * k + 1]
        x_ref[0:rows, :] = pre_ref[hidden:, :] + dot_nn(wbs_ref[...], grad_ref[0 : hidden + rows, cols[k]])

    def give(k):
        x_ref = scratch[4 * k]
        for f in range(fields):
            demb_ref[f, :, cols[k]] = x_ref[emb * f : emb * f + PAD, :].astype(BF16)
        dg_ref[:, cols[k]] = x_ref[cat:full, :] * dm_ref[:, cols[k]].astype(F32)

    dlogits = {}
    for phase, k in ORDER[tiles]:
        if phase == "w":
            pl.when(start)(loads[k].wait)
        elif phase == "x":
            gather(k)
        elif phase == "f":
            forward(k)
        elif phase == "l":
            dlogits[k] = logits(k)
        elif phase == "g":
            gradients(k, dlogits[k])
        elif phase == "b":
            backward(k)
        else:
            give(k)

    @pl.when(pl.program_id(0) == pl.num_programs(0) - 1)
    def _():
        each = jnp.zeros((8, 128), F32)
        for ref in (hca_ref, hda_ref, sc_ref):
            each = peak(each, ref[...])
        heads = jnp.zeros((8, 128), F32)
        for ref, most in ((hc_ref, X_TOP), (hd_ref, SLOPE_TOP)):
            heads = jnp.maximum(heads, most * peak(jnp.zeros((8, 128), F32), ref[...]))
        products = jnp.max(jnp.max(heads, axis=1, keepdims=True), axis=0, keepdims=True) * (
            X_TOP * tiles * TILE * pl.num_programs(0)
        )
        products = products * jnp.maximum(top_ref[:, 0:128], top_ref[:, 128:256])
        expo_ref[...] = exponents(jnp.maximum(each * 128.0, products))


ORDER = {
    2: [
        ("x", 0), ("x", 1), ("w", 0), ("f", 0), ("f", 1), ("l", 0), ("w", 1), ("l", 1),
        ("g", 0), ("b", 0), ("g", 1), ("b", 1), ("o", 0), ("o", 1),
    ],
}


TILES = 2


def layers(chunks, dense_values, dense_present, labels, weights, columns, emb, scale):
    fields = sum(c.shape[0] for c in chunks)
    dense, examples = dense_values.shape
    hidden = columns[1].shape[0]
    rows = columns[0].shape[0]
    tall = ceil_to(rows, 16)
    take = TILES * TILE
    column = lambda r: pl.BlockSpec((r, take), lambda t: (0, t))
    whole = lambda a: pl.BlockSpec(a.shape, lambda t: (0,) * a.ndim, pipeline_mode=pl.Buffered(1))
    kept = lambda r: pl.BlockSpec((r, 128), lambda t: (0, 0))
    shape = jax.ShapeDtypeStruct
    return pl.pallas_call(
        lambda *refs: layers_kernel((fields, emb, dense, len(chunks), TILES), scale, *refs),
        grid=(examples // take,),
        in_specs=[pl.BlockSpec((c.shape[0], PAD, take), lambda t: (0, 0, t)) for c in chunks]
        + [column(dense), column(dense), column(1)]
        + [pl.BlockSpec(memory_space=pltpu.HBM) for _ in weights]
        + [whole(a) for a in columns],
        out_specs=[
            column(1),
            column(tall),
            column(hidden + tall),
            pl.BlockSpec((fields, PAD, take), lambda t: (0, 0, t)),
            column(dense),
            kept(rows),
            kept(hidden),
            kept(8),
            kept(8),
        ],
        out_shape=[
            shape((1, examples), F32),
            shape((tall, examples), BF16),
            shape((hidden + tall, examples), BF16),
            shape((fields, PAD, examples), BF16),
            shape((dense, examples), F32),
            shape((rows, 128), F32),
            shape((hidden, 128), F32),
            shape((8, 128), F32),
            shape((8, 128), F32),
        ],
        scratch_shapes=[pltpu.VMEM((8, TILE), F32)]
        + [pltpu.VMEM(w.shape, BF16) for w in weights]
        + [pltpu.SemaphoreType.DMA((2,))]
        + [
            pltpu.VMEM((tall, TILE), F32),
            pltpu.VMEM((rows + hidden, TILE), F32),
            pltpu.VMEM((hidden, TILE), F32),
            pltpu.VMEM((hidden, TILE), F32),
        ]
        * TILES,
        compiler_params=params(40),
        cost_estimate=cost(2 * examples * rows * (2 * rows + 2 * hidden), 9 * 2**20 + 20 * rows * examples),
        name="layers",
    )(*chunks, dense_values, dense_present, labels, *map(in_hbm, weights), *columns)


def weight_kernel(rows, examples_all, half_ref, *refs):
    xa_ref, dd_ref, dc_ref, dct_ref, hc_ref, hct_ref, hd_ref, sc_ref, expo_ref, out_ref, over = refs
    quarter = out_ref.shape[2] - FRONT
    half, j = half_ref[0], pl.program_id(0)
    first = half * pl.num_programs(0) + j == 0
    x = xa_ref[0:rows, :]
    hidden = over.shape[1] - 128

    @pl.when(j == 0)
    def _():
        tail = dot_nt(x, dct_ref[...])
        tail = jnp.concatenate([tail, jnp.zeros((rows, 128 - 16), F32)], axis=1)
        for r in range(0, hidden, 128):
            over[:, r : r + 128] = tail[r : r + 128].T[0:8]
        last = jnp.concatenate([tail[hidden:rows], jnp.zeros((128 - rows + hidden, 128), F32)], axis=0)
        over[:, hidden:] = last.T[0:8]

    deep = dot_nt(x, dd_ref[...])
    cross = dot_nt(x, dc_ref[...])
    at = pl.multiple_of((half * pl.num_programs(0) + j) * TILE, TILE)
    total = lambda ref: jnp.sum(ref[...].T, axis=0, keepdims=True)
    row = lax.broadcasted_iota(jnp.int32, (8, TILE), 0)
    heads = jnp.where(row == 0, total(hc_ref), jnp.where(row == 1, total(hd_ref), 0.0))
    zeros = lambda n, m: jnp.zeros((n, m), F32)
    corner = jnp.concatenate([over[0:3, hidden:], zeros(3, TILE - 128)], axis=1)
    small = jnp.concatenate([zeros(2, TILE), corner, zeros(3, TILE)], axis=0)
    ends = jnp.concatenate([hct_ref[...], zeros(120, 128)], axis=0)
    ends = jnp.concatenate([total(ends), zeros(1, TILE - 128)], axis=1)
    sums = jnp.sum(sc_ref[...], axis=1, keepdims=True)
    lane = lax.broadcasted_iota(jnp.int32, (8, TILE), 1)
    scalars = jnp.where(lane == 0, sums[0:1] / examples_all, jnp.where(lane == 1, sums[1:2], 0.0))
    small = small + jnp.where(row == 5, ends, 0.0) + jnp.where(row == 6, scalars, 0.0)
    heads = heads + jnp.where(first, small, 0.0)
    parts = [(0, deep), (rows, cross), (2 * rows, over[:, pl.ds(at, TILE)]), (2 * rows + 8, heads)]
    for q in range(4):
        for h in range(2):
            out_ref[q, h, 0:FRONT, :] = expo_ref[...]
    for base, part in parts:
        at = 0
        while at < part.shape[0]:
            q, r = divmod(base + at, quarter)
            n = min(part.shape[0] - at, quarter - r)
            place = jnp.where(half == 0, (0, 2, 1, 3)[q], q)
            for h in range(2):
                out_ref[place, h, FRONT + r : FRONT + r + n, :] = part[at : at + n, h * 128 : (h + 1) * 128]
            at += n


def weight_grads(half, xa, grads, hca, hda, sc, expo, examples_all):
    tall, examples = xa.shape
    rows, hidden = hca.shape[0], hda.shape[0]
    quarter = ceil_to(2 * rows + 16, 32) // 4
    steps = hidden // TILE // 2
    return pl.pallas_call(
        lambda *refs: weight_kernel(rows, examples_all, *refs),
        grid_spec=pltpu.PrefetchScalarGridSpec(
            num_scalar_prefetch=1,
            grid=(steps,),
            in_specs=[
                pl.BlockSpec((tall, examples), lambda j, h: (0, 0), pipeline_mode=pl.Buffered(1)),
                pl.BlockSpec((TILE, examples), lambda j, h: (h[0] * steps + j, 0)),
                pl.BlockSpec((TILE, examples), lambda j, h: (2 * steps + h[0] * steps + j, 0)),
                pl.BlockSpec((16, examples), lambda j, h: (2 * hidden // 16, 0)),
                pl.BlockSpec((TILE, 128), lambda j, h: (h[0] * steps + j, 0)),
                pl.BlockSpec((8, 128), lambda j, h: (hidden // 8, 0)),
                pl.BlockSpec((TILE, 128), lambda j, h: (h[0] * steps + j, 0)),
                pl.BlockSpec((8, 128), lambda j, h: (0, 0)),
                pl.BlockSpec((8, 128), lambda j, h: (0, 0)),
            ],
            out_specs=pl.BlockSpec((4, 2, FRONT + quarter, 128), lambda j, h: (0, j, 0, 0)),
            scratch_shapes=[pltpu.VMEM((8, hidden + 128), F32)],
        ),
        out_shape=jax.ShapeDtypeStruct((4, 2 * steps, FRONT + quarter, 128), F32),
        compiler_params=params(16),
        cost_estimate=cost(2 * examples * rows * hidden, 10 * rows * hidden),
        name="weight_grads",
    )(half.reshape(1).astype(jnp.int32), xa, *[in_hbm(grads)] * 3, *map(in_hbm, (hca, hca, hda)), sc, expo)


def spread_kernel(first, core_ref, place_ref, block_ref, own_ref, sib_ref, out_ref, expo_ref, top_ref):
    count, _, examples = own_ref.shape
    n_blocks = out_ref.shape[0] * out_ref.shape[1]

    @pl.when(pl.program_id(0) == 0)
    def _():
        top_ref[...] = jnp.zeros_like(top_ref)

    core = core_ref[0]
    every = []
    for k in range(count):
        f = first + pl.program_id(0) * count + k
        sums = jnp.zeros((n_blocks * PAD, HI), F32)
        for s, ref in enumerate((own_ref, sib_ref)):
            base = (core if s == 0 else 1 - core) * examples
            for at in range(0, examples, WIDE):
                cols = pl.ds(pl.multiple_of(base + at, WIDE), WIDE)
                place = place_ref[pl.ds(f, 1), cols]
                block = block_ref[pl.ds(f, 1), cols]
                grads = ref[k, :, at : at + WIDE].astype(F32)
                chosen = [jnp.where(block == b, grads, 0.0) for b in range(n_blocks)]
                chosen = jnp.concatenate(chosen, axis=0).astype(BF16)
                sums = sums + dot_nt(chosen, onehot_rows(place, WIDE))
        every.append(sums)
    for k, sums in enumerate(every):
        top_ref[...] = peak(top_ref[...], sums)
        for b in range(n_blocks):
            for h in range(2):
                out_ref[b // out_ref.shape[1], b % out_ref.shape[1], h, k * PAD : (k + 1) * PAD] = sums[
                    b * PAD : (b + 1) * PAD, h * 128 : (h + 1) * 128
                ]

    @pl.when(pl.program_id(0) == pl.num_programs(0) - 1)
    def _():
        expo_ref[...] = exponents(jnp.maximum(top_ref[:, 0:128], top_ref[:, 128:256]))


def spread(core, place, block, own, sib, first, count, blocks):
    fields, _, examples = own.shape
    whole = lambda a: pl.BlockSpec(a.shape, lambda f: (0, 0), pipeline_mode=pl.Buffered(1))
    take = 2
    return pl.pallas_call(
        lambda *refs: spread_kernel(first, *refs),
        grid=(count // take,),
        in_specs=[pl.BlockSpec(memory_space=pltpu.SMEM), whole(place), whole(block)]
        + [pl.BlockSpec((take, PAD, examples), lambda f: (f + first // take, 0, 0))] * 2,
        out_specs=[
            pl.BlockSpec((2, blocks, 2, take * PAD, 128), lambda f: (0, 0, 0, f, 0)),
            pl.BlockSpec((8, 128), lambda f: (0, 0)),
        ],
        out_shape=[
            jax.ShapeDtypeStruct((2, blocks, 2, count * PAD, 128), F32),
            jax.ShapeDtypeStruct((8, 128), F32),
        ],
        scratch_shapes=[pltpu.VMEM((8, HI), F32)],
        compiler_params=params(10),
        cost_estimate=cost(8 * count * blocks * PAD * HI * examples, 4 * count * PAD * 16 * 128 * blocks),
        name="spread",
    )(core.reshape(1).astype(jnp.int32), place, block, own, sib)


def flip(array, axis, bit):
    size = lax.axis_size(axis)
    return lax.ppermute(array, axis, [(i, i ^ (1 << bit)) for i in range(size)])


def bit_of(axis, bit):
    return (lax.axis_index(axis) >> bit) & 1


def crossed_pairs(stage, n_dp, n_mp):
    pairs = []
    for d in range(n_dp):
        for m in range(n_mp):
            along_dp = (m & 1) == stage
            to = (d ^ 1, m) if along_dp else (d, m ^ 2)
            pairs.append((d * n_mp + m, to[0] * n_mp + to[1]))
    return pairs


def crossed_flip(array, stage):
    return lax.ppermute(array, ("dp", "mp"), crossed_pairs(stage, lax.axis_size("dp"), lax.axis_size("mp")))


def crossed_bit(stage):
    return jnp.where(bit_of("mp", 0) == stage, bit_of("dp", 0), bit_of("mp", 1))


def after(value, token):
    return lax.optimization_barrier((value, token))[0]


def encode(values, expo, at):
    row = lax.broadcasted_iota(jnp.int32, values.shape, values.ndim - 2)
    here = expo.reshape((1,) * (values.ndim - 1) + (128,))
    return jnp.where(row == at, here, values * jnp.exp2(-here)).astype(F16)


def add(kept, expo, got, at):
    theirs = got[(0,) * (got.ndim - 2) + (at,)].astype(F32)
    total = kept + got.astype(F32) * jnp.exp2(theirs).reshape((1,) * (got.ndim - 1) + (128,))
    return total, jnp.maximum(expo, theirs) + 1.0


def block_of(acc, *index):
    start = (*index, *(0,) * (acc.ndim - len(index)))
    block = lax.dynamic_slice(acc, start, (1,) * len(index) + acc.shape[len(index) :])
    return block.reshape(acc.shape[len(index) :])


def decode(got, at):
    theirs = got[(0,) * (got.ndim - 2) + (at,)].astype(F32)
    return got.astype(F32) * jnp.exp2(theirs).reshape((1,) * (got.ndim - 1) + (128,)), theirs


def reduction(acc, expo, at, z_dim):
    (first, send_first), (second, send_second), *rest = stages()
    ahead = encode(block_of(acc, 1 - first, 1 - second), expo, at)
    got_ahead = send_first(ahead)
    behind = encode(block_of(acc, 1 - first, second), expo, at)
    got_behind = send_first(behind)
    token = yield ahead, behind
    more, theirs = decode(after(got_ahead, token), at)
    expo = jnp.maximum(expo, theirs) + 1.0
    message = encode(block_of(acc, first, 1 - second) + more, expo, at)
    got = send_second(message)
    token = yield message
    got, got_behind = after((got, got_behind), token)
    more, theirs = decode(got, at)
    acc = block_of(acc, first, second) + decode(got_behind, at)[0] + more
    expo = jnp.maximum(expo, theirs) + 1.0
    acc = jnp.swapaxes(acc.reshape(2, 2, *acc.shape[z_dim:]), 0, 1)
    for mine, send in rest:
        message = encode(block_of(acc, 1 - mine), expo, at)
        got = send(message)
        token = yield message
        more, theirs = decode(after(got, token), at)
        acc, expo = block_of(acc, mine) + more, jnp.maximum(expo, theirs) + 1.0
    yield acc, expo


def gathering(piece, scale, core):
    (first, send_first), (second, send_second), *rest = stages()
    to_sibling = lambda a: flip(a, "mp", 0)
    every = jnp.zeros((2, 2, 2, 2, 2, *piece.shape), F32)

    def place(every, values, *index):
        values = (values.astype(F32) * scale)[None, None, None]
        return lax.dynamic_update_slice(every, values, (*index, *(0,) * (every.ndim - 3)))

    for mine, send in reversed(rest):
        other = send(piece)
        token = yield piece
        other = after(other, token)
        low = mine == 0
        piece = jnp.stack([jnp.where(low, piece, other), jnp.where(low, other, piece)], axis=0)
    by_second, by_first, sib = send_second(piece), send_first(piece), to_sibling(piece)
    every = place(every, piece, core, first, second)
    token = yield piece
    by_second = after(by_second, token)
    by_both, sib_second = send_first(by_second), to_sibling(by_second)
    by_first = after(by_first, by_second)
    sib_first = to_sibling(by_first)
    every = place(every, by_second, core, first, 1 - second)
    every = place(every, by_first, core, 1 - first, second)
    every = place(every, after(sib, token), 1 - core, second, first)
    token = yield by_first
    by_both = after(by_both, token)
    sib_both = to_sibling(by_both)
    every = place(every, by_both, core, 1 - first, 1 - second)
    every = place(every, sib_second, 1 - core, second, 1 - first)
    every = place(every, sib_first, 1 - core, 1 - second, first)
    every = place(every, sib_both, 1 - core, 1 - second, 1 - first)
    yield every


def stages():
    return [
        (crossed_bit(0), lambda a: crossed_flip(a, 0)),
        (crossed_bit(1), lambda a: crossed_flip(a, 1)),
        (bit_of("dp", 1), lambda a: flip(a, "dp", 1)),
        (bit_of("dp", 2), lambda a: flip(a, "dp", 2)),
    ]


def assemble_kernel(rows, full, in_ref, over_ref, cross_ref, deep_ref, vec_ref):
    t = pl.program_id(0)
    last = pl.num_programs(0) - 1

    @pl.when(t < last)
    def _():
        for h in range(2):
            cols = slice(h * 128, (h + 1) * 128)
            parts = []
            for q in range(4):
                ahead = jnp.where(t < last // 2, q % 2, q // 2)
                parts.append(in_ref[0, ahead, q // 2 + q % 2 - ahead, h, 0, FRONT:, :])
            every = jnp.concatenate(parts, axis=0)
            deep_ref[:, cols] = every[0:full]
            cross_ref[:, cols] = every[rows : rows + full]
            vec_ref[0:1, cols] = every[rows + full : rows + full + 1]
            vec_ref[1:2, cols] = every[full : full + 1]
            vec_ref[2:4, cols] = every[2 * rows + 8 : 2 * rows + 10]
            vec_ref[4:8, cols] = every[2 * rows + 12 : 2 * rows + 16]

    @pl.when(t == last)
    def _():
        cross_ref[:, 0:128] = over_ref[0:full, :]


def assemble(pieces, rows, full, hidden):
    steps = hidden // 256
    quarter = pieces.shape[5] - FRONT
    half = steps // 2
    spare = pieces[:, 1, 1, :, :, FRONT + quarter - 16 :, :].transpose(3, 0, 2, 1, 4).reshape(16, hidden)
    extra = full - hidden
    over = jnp.concatenate([spare[0:extra], spare[10 : 10 + extra, 0 : rows - hidden]], axis=1)
    over = jnp.pad(over.T, ((0, 0), (0, 128 - extra)))
    now = lambda t: jnp.minimum(t, steps - 1)
    return pl.pallas_call(
        lambda *refs: assemble_kernel(rows, full, *refs),
        grid=(steps + 1,),
        in_specs=[
            pl.BlockSpec(
                (1, 2, 2, 2, 1, FRONT + quarter, 128), lambda t: (now(t) // half, 0, 0, 0, now(t) % half, 0, 0)
            ),
            pl.BlockSpec((rows, 128), lambda t: (0, 0)),
        ],
        out_specs=[
            pl.BlockSpec((full, 256), lambda t: (0, t)),
            pl.BlockSpec((full, 256), lambda t: (0, now(t))),
            pl.BlockSpec((8, 256), lambda t: (0, now(t))),
        ],
        out_shape=[
            jax.ShapeDtypeStruct((full, full), F32),
            jax.ShapeDtypeStruct((full, hidden), F32),
            jax.ShapeDtypeStruct((8, hidden), F32),
        ],
        compiler_params=params(10),
        cost_estimate=cost(0, 16 * rows * hidden),
        name="assemble",
    )(in_vmem(pieces), over), over


def table_place(ids, table_rows, n_dp, core):
    upper = ids // (2 * table_rows)
    rest = ids % table_rows
    if n_dp == 8:
        piece = table_rows // n_dp
        at = rest // piece
        low = at % 2
        first = jnp.where(core == 0, low, upper)
        second = jnp.where(core == 0, upper, low)
        block = first * 4 + second * 2 + at // 4
        place = (at // 2) % 2 * piece + rest % piece
    else:
        block = upper * (table_rows // HI) + rest // HI
        place = rest % HI
    return place, jnp.where((ids // table_rows) % 2 == core, block, -1)


def body(
    field_ids,
    field_present,
    dense_values,
    dense_present,
    clicked,
    tables,
    cross_weight,
    cross_bias,
    deep_weight,
    deep_bias,
    head_cross,
    head_deep,
    head_bias,
):
    fields, batch_group = field_ids.shape
    table_rows, cat = tables.shape
    emb = cat // fields
    full, hidden = deep_weight.shape
    dense = full - cat
    n_dp, n_mp = lax.axis_size("dp"), lax.axis_size("mp")
    examples = batch_group // n_mp
    examples_all = batch_group * n_dp
    blocks = table_rows // HI
    rows = ceil_to(full + 1, 8)
    me = lax.axis_index("mp")
    core = me & 1

    chosen = jnp.where(field_present > 0, field_ids, 0)
    own_ids = lax.dynamic_slice_in_dim(chosen, me * examples, examples, 1)
    place_own = own_ids & (HI - 1)
    block_own = (own_ids // HI) ^ (me * blocks)
    pair_ids = lax.dynamic_slice_in_dim(chosen, (me - core) * examples, 2 * examples, 1)
    place, block = table_place(pair_ids, table_rows, n_dp, core)

    columns = tables.T
    cuts = [(0, CUTS[0]), CUTS, (CUTS[1], fields)]
    far = [columns[a * emb : b * emb] for a, b in cuts[:2]]
    first_weight = after(cross_weight, far)
    weights = prepare(first_weight, deep_weight, cross_bias, deep_bias, head_cross, head_deep, rows)
    far.append(after(columns, weights[0])[cuts[2][0] * emb :])
    far = [flip(part, "mp", 1) for part in far]
    near = flip(columns, "mp", 0)
    place, block = after((place, block), weights[0])
    token = place, block
    found = []
    for k, (a, b) in enumerate(cuts):
        far_near = flip(after(far[k], token), "mp", 0)
        found.append(lookup(place_own[a:b], block_own[a:b], (columns, near, far[k], far_near), a * emb, emb))
        token = found[-1]

    logit, xa, grads, demb, dense_grad, hca, hda, sc, expo = layers(
        found,
        dense_values,
        dense_present,
        clicked[None, :],
        weights[:2],
        (*weights[2:], jnp.broadcast_to(head_bias[:, None], (8, 128))),
        emb,
        1.0 / math.sqrt(examples_all),
    )
    demb_sib = flip(demb, "mp", 0)
    grad_args = (xa, grads, hca, hda, sc, expo, examples_all)
    away = weight_grads(1 - core, *grad_args)
    if n_dp == 8:
        away = encode(away, expo[0], FRONT - 1)
    got = flip(away, "mp", 0)
    sums = weight_grads(after(core, away), *grad_args)
    halves = [(0, 12), (12, fields)]

    def table_part(token, k):
        a, b = halves[k]
        part, top = spread(core, place, block, after(demb, token), demb_sib, a, b - a, blocks)
        return part, top[0]

    if n_dp == 8:
        got = after(got, sums)
        both, expo = add(sums, expo[0], got, FRONT - 1)
        both = both.reshape(2, 2, *sums.shape[1:])
        weight_chain = reduction(both, expo, FRONT - 1, 1)
        token = next(weight_chain)
        table_chains = []
        for k in range(2):
            part, top = table_part(token, k)
            part = part.reshape(2, 2, 2, 2, *part.shape[3:])
            table_chains.append(reduction(part, top, PAD - 1, 2))
            token = weight_chain.send(part)
            token = token, next(table_chains[k])
        chain = {"w": weight_chain, "a": table_chains[0], "b": table_chains[1]}
        table_out, total = {}, None
        for name in "awbawwabwabwbw":
            token = chain[name].send(token)
            if name == "w" and total is None and isinstance(token, tuple):
                total, expo = token
                total = (total * jnp.exp2(-expo)[None, :]).astype(F16)
                chain["w"] = gathering(total, jnp.exp2(expo), core)
                token = next(chain["w"])
            elif name != "w" and isinstance(token, tuple):
                token = table_out[name] = token[0]
        pieces = token
        table_out = jnp.concatenate([table_out["a"], table_out["b"]], axis=0)
    else:
        summed = lax.psum(sums + got, "dp")
        summed = summed + flip(summed, "mp", 1)
        pieces = lax.all_gather(summed, "mp")[0:2].reshape(2, 2, 2, 2, 2, *sums.shape[2:])
        pieces = jnp.swapaxes(pieces, 3, 4)
        table_out = jnp.concatenate([table_part(sums, k)[0] for k in range(2)], axis=3)
        table_out = table_out.transpose(0, 3, 1, 2, 4).reshape(2, fields * PAD, table_rows)
        upper = bit_of("mp", 1)
        away = lax.dynamic_index_in_dim(table_out, 1 - upper, 0, keepdims=False)
        table_out = lax.dynamic_index_in_dim(table_out, upper, 0, keepdims=False) + flip(away, "mp", 1)
        table_out = lax.psum_scatter(table_out, "dp", scatter_dimension=1, tiled=True)
    tables_grad = table_out.reshape(fields, PAD, -1)[:, :emb].reshape(cat, -1).T
    (cross_grad, deep_grad, small), over = assemble(pieces, rows, full, hidden)
    return (
        logit[0],
        small[6, 0],
        dense_grad,
        tables_grad,
        cross_grad,
        jnp.concatenate([small[0], over[full, 0 : full - hidden]]),
        deep_grad,
        small[1],
        jnp.concatenate([small[2], small[5, 0 : full - hidden]]),
        small[3],
        small[6, 1:2],
    )


def solution(mesh):
    placed = (
        P(None, "dp"),
        P(None, "dp"),
        P(None, ("dp", "mp")),
        P(None, ("dp", "mp")),
        P(("dp", "mp")),
        P("mp", None),
        P(),
        P(),
        P(),
        P(),
        P(),
        P(),
        P(),
    )
    return jax.shard_map(
        body,
        mesh=mesh,
        in_specs=placed,
        out_specs=(
            P(("dp", "mp")),
            P(),
            P(None, ("dp", "mp")),
            P(("mp", "dp"), None),
            P(),
            P(),
            P(),
            P(),
            P(),
            P(),
            P(),
        ),
        check_vma=False,
    )
```

```python
import math

import jax
import jax.numpy as jnp
from jax import lax
from jax.experimental import pallas as pl
from jax.experimental.pallas import tpu as pltpu
from jax.sharding import PartitionSpec as P

BF16, F32, F16 = jnp.bfloat16, jnp.float32, jnp.float16
HI = 256
ONES = 3
SLOPE_TOP = 1.25
X_TOP = 6.0
FRONT = 8
PAD = 40
TILE = 256
CUTS = (13, 22)
WIDE = 512
GELU_S = math.sqrt(2.0 / math.pi)
GELU_C = 0.044715


def params(mebibytes):
    return pltpu.CompilerParams(vmem_limit_bytes=mebibytes * 1024 * 1024)


def cost(flops, moved):
    return pl.CostEstimate(flops=int(flops), bytes_accessed=int(moved), transcendentals=0)


def in_hbm(array):
    return pltpu.with_memory_space_constraint(array, pltpu.HBM)


def in_vmem(array):
    return pltpu.with_memory_space_constraint(array, pltpu.VMEM)


def ceil_to(value, unit):
    return -(-value // unit) * unit


def dot_nn(left, right):
    return jnp.dot(left, right, preferred_element_type=F32)


def dot_nt(left, right, precision=None):
    return lax.dot_general(
        left, right, (((1,), (1,)), ((), ())), preferred_element_type=F32, precision=precision
    )


def onehot_rows(place, width):
    rows = lax.broadcasted_iota(jnp.int16, (HI, width), 0)
    return jnp.where(rows == place.astype(jnp.int16), jnp.ones((), BF16), jnp.zeros((), BF16))


def prepare_kernel(cw_ref, dw_ref, cb_ref, db_ref, hc_ref, hd_ref, ww_ref, wb_ref, hco_ref, hdo_ref, pad):
    full, hidden = dw_ref.shape
    rows = wb_ref.shape[0]
    pad[...] = jnp.zeros_like(pad)
    for source, bias, more, base, width in ((dw_ref, db_ref, 0.0, 0, hidden), (cw_ref, cb_ref, 1.0, hidden, full)):
        pad[0:full, 0:width] = source[...].astype(F32)
        rest = bias[:, 0:width] + more
        for k in range(ONES):
            part = rest.astype(BF16).astype(F32)
            pad[full + k : full + k + 1, 0:width] = part
            rest = rest - part
        if width < rows:
            pad[:, width:] = jnp.zeros((pad.shape[0], pad.shape[1] - width), F32)
        wide_width = hidden if base == 0 else rows
        wb_ref[:, base : base + wide_width] = pad[0:rows, 0:wide_width].astype(BF16)
        for r in range(0, wide_width, 128):
            n = min(128, wide_width - r)
            turned = pad[:, r : r + 128].T
            ww_ref[base + r : base + r + n, :] = turned[0:n, 0:rows].astype(BF16)
    for source, out in ((hc_ref, hco_ref), (hd_ref, hdo_ref)):
        for r in range(0, out.shape[0], 128):
            n = min(128, out.shape[0] - r)
            line = source[:, r : r + 128]
            out[r : r + n, :] = jnp.broadcast_to(line, (128, 128)).T[0:n]


def prepare(cross_weight, deep_weight, cross_bias, deep_bias, head_cross, head_deep, rows):
    full, hidden = deep_weight.shape
    wide_rows = ceil_to(rows, 128)
    line = lambda v: jnp.pad(v, (0, ceil_to(v.shape[0], 128) - v.shape[0]))[None, :]
    shape = jax.ShapeDtypeStruct
    return pl.pallas_call(
        prepare_kernel,
        out_shape=[
            shape((hidden + rows, rows), BF16),
            shape((rows, hidden + rows), BF16),
            shape((rows, 128), F32),
            shape((hidden, 128), F32),
        ],
        scratch_shapes=[pltpu.VMEM((wide_rows, wide_rows), F32)],
        compiler_params=params(16),
        cost_estimate=cost(0, 16 * rows * rows),
        name="prepare",
    )(cross_weight, deep_weight, line(cross_bias), line(deep_bias), line(head_cross), line(head_deep))


def lookup_kernel(emb, blocks, at_row, place_ref, block_ref, *refs):
    sources, out_ref, flat, packed = refs[0:4], refs[4], refs[5], refs[6]
    n_fields, examples = place_ref.shape
    rows = emb * n_fields
    for s, source in enumerate(sources):
        first = at_row if s < 2 else 0
        flat[s, 0:rows, :] = source[first : first + rows, :].astype(F32)
    for f in range(n_fields):
        for s in range(4):
            for b in range(blocks):
                piece = flat[s, emb * f : emb * f + PAD, b * HI : (b + 1) * HI]
                at = (s * blocks + b) * PAD
                packed[f, at : at + PAD, :] = piece.astype(BF16)

    for f in range(n_fields):
        block = block_ref[f : f + 1, :]
        found = dot_nn(packed[f], onehot_rows(place_ref[f : f + 1, :], examples))
        acc = found[0:PAD]
        for b in range(1, 4 * blocks):
            acc = jnp.where(block == b, found[b * PAD : (b + 1) * PAD], acc)
        out_ref[f] = acc.astype(BF16)


def lookup(place, block, sources, at_row, emb):
    n_fields, examples = place.shape
    width = sources[0].shape[1]
    blocks = width // HI
    n_rows = 4 * blocks * PAD
    return pl.pallas_call(
        lambda *refs: lookup_kernel(emb, blocks, at_row, *refs),
        out_shape=jax.ShapeDtypeStruct((n_fields, PAD, examples), BF16),
        scratch_shapes=[
            pltpu.VMEM((4, ceil_to(n_fields * emb, 8) + 8, width), F32),
            pltpu.VMEM((n_fields, n_rows, HI), BF16),
        ],
        compiler_params=params(16),
        cost_estimate=cost(2 * n_fields * n_rows * HI * examples, 4 * n_fields * PAD * examples),
        name="lookup",
    )(place, block, *sources)


def wide(column, width):
    return jnp.concatenate([column] * (width // 128), axis=1)


def fold(values):
    total = values[:, 0:128]
    for at in range(128, values.shape[1], 128):
        total = total + values[:, at : at + 128]
    return total


def peak(top, values):
    for r in range(0, values.shape[0], 8):
        top = jnp.maximum(top, jnp.abs(values[r : r + 8]))
    return top


def exponents(top):
    most = jnp.max(jnp.max(top, axis=1, keepdims=True), axis=0, keepdims=True)
    return jnp.broadcast_to(jnp.ceil(jnp.log(jnp.maximum(most, 1e-30)) * (1.0 / math.log(2.0))) - 14.0, (8, 128))


def layers_kernel(sizes, scale, *refs):
    fields, emb, dense, n_chunks, tiles = sizes
    chunks = refs[:n_chunks]
    (dv_ref, dm_ref, lab_ref, ww_ref, wb_ref, hc_ref, hd_ref, hb_ref) = refs[n_chunks : n_chunks + 8]
    (logit_ref, xa_ref, grad_ref, demb_ref, dg_ref, hca_ref, hda_ref, sc_ref, expo_ref) = refs[
        n_chunks + 8 : n_chunks + 17
    ]
    top_ref, wws_ref, wbs_ref, sems, *scratch = refs[n_chunks + 17 :]
    loads = [
        pltpu.make_async_copy(ww_ref, wws_ref, sems.at[0]),
        pltpu.make_async_copy(wb_ref, wbs_ref, sems.at[1]),
    ]
    start = pl.program_id(0) == 0
    hidden = hda_ref.shape[0]
    rows = hca_ref.shape[0]
    width = TILE
    cat = fields * emb
    full = cat + dense
    step = 128
    cuts = [(a, min(a + step, rows)) for a in range(0, rows, step)]
    hid_cuts = [(a, min(a + step, hidden)) for a in range(0, hidden, step)]
    cols = [slice(k * TILE, (k + 1) * TILE) for k in range(tiles)]
    tall = xa_ref.shape[0]

    @pl.when(start)
    def _():
        for load in loads:
            load.start()
        hca_ref[...] = jnp.zeros_like(hca_ref)
        hda_ref[...] = jnp.zeros_like(hda_ref)
        sc_ref[...] = jnp.zeros_like(sc_ref)
        top_ref[...] = jnp.zeros_like(top_ref)

    def gather(k):
        x_ref = scratch[4 * k]
        f = 0
        for chunk in chunks:
            for c in range(chunk.shape[0]):
                x_ref[emb * f : emb * f + PAD, :] = chunk[c, :, cols[k]].astype(F32)
                f += 1
        x_ref[cat:full, :] = dv_ref[:, cols[k]] * dm_ref[:, cols[k]].astype(F32)
        x_ref[full:tall, :] = (
            lax.broadcasted_iota(jnp.int32, (tall - full, width), 0) < ONES
        ).astype(F32)
        xa_ref[:, cols[k]] = x_ref[0:tall, :].astype(BF16)

    def forward(k):
        scratch[4 * k + 1][...] = dot_nn(wws_ref[...], xa_ref[0:rows, cols[k]])

    def logits(k):
        x_ref, pre_ref, act_ref, slope_ref = scratch[4 * k : 4 * k + 4]
        total = jnp.zeros((8, width), F32)
        for a, b in cuts:
            cp = pre_ref[hidden + a : hidden + b, :]
            term = (x_ref[a:b, :] * cp) * wide(hc_ref[a:b, :], width)
            for r in range(0, b - a, 8):
                total = total + term[r : r + 8]
        for a, b in hid_cuts:
            v = pre_ref[a:b, :]
            vv = v * v
            half = 0.5 + 0.5 * jnp.tanh(v * (GELU_S + (GELU_S * GELU_C) * vv))
            act = v * half
            act_ref[a:b, :] = act
            slope_ref[a:b, :] = half + (act * (1.0 - half)) * ((2.0 * GELU_S) + (6.0 * GELU_S * GELU_C) * vv)
            term = act * wide(hd_ref[a:b, :], width)
            for r in range(0, b - a, 8):
                total = total + term[r : r + 8]
        logit = jnp.sum(total, axis=0, keepdims=True) + hb_ref[0:1, 0:1]
        logit_ref[:, cols[k]] = logit
        labels = lab_ref[:, cols[k]].astype(F32)
        small = jnp.exp(-jnp.abs(logit))
        loss = jnp.maximum(logit, 0.0) + jnp.log1p(small) - labels * logit
        sig = jnp.where(logit >= 0.0, 1.0, small) / (1.0 + small)
        dlogit = (sig - labels) * scale
        sc_ref[0:1, :] += fold(loss)
        sc_ref[1:2, :] += fold(dlogit)
        top_ref[...] = jnp.maximum(top_ref[...], jnp.abs(dlogit))
        return dlogit

    def gradients(k, dlogit):
        x_ref, pre_ref, act_ref, slope_ref = scratch[4 * k : 4 * k + 4]
        for a, b in hid_cuts:
            hda_ref[a:b, :] += fold(dlogit * act_ref[a:b, :])
            dd = (dlogit * wide(hd_ref[a:b, :], width)) * slope_ref[a:b, :]
            grad_ref[a:b, cols[k]] = dd.astype(BF16)
        for a, b in cuts:
            cp = pre_ref[hidden + a : hidden + b, :]
            dx = dlogit * x_ref[a:b, :]
            hc = wide(hc_ref[a:b, :], width)
            hca_ref[a:b, :] += fold(dx * cp)
            dc = dx * hc
            if b == rows:
                dc = jnp.concatenate([dc, jnp.zeros((tall - rows, width), F32)], axis=0)
            grad_ref[hidden + a : hidden + a + dc.shape[0], cols[k]] = dc.astype(BF16)
            pre_ref[hidden + a : hidden + b, :] = (dlogit * hc) * cp

    def backward(k):
        x_ref, pre_ref = scratch[4 * k], scratch[4 * k + 1]
        x_ref[0:rows, :] = pre_ref[hidden:, :] + dot_nn(wbs_ref[...], grad_ref[0 : hidden + rows, cols[k]])

    def give(k):
        x_ref = scratch[4 * k]
        for f in range(fields):
            demb_ref[f, :, cols[k]] = x_ref[emb * f : emb * f + PAD, :].astype(BF16)
        dg_ref[:, cols[k]] = x_ref[cat:full, :] * dm_ref[:, cols[k]].astype(F32)

    dlogits = {}
    for phase, k in ORDER[tiles]:
        if phase == "w":
            pl.when(start)(loads[k].wait)
        elif phase == "x":
            gather(k)
        elif phase == "f":
            forward(k)
        elif phase == "l":
            dlogits[k] = logits(k)
        elif phase == "g":
            gradients(k, dlogits[k])
        elif phase == "b":
            backward(k)
        else:
            give(k)

    @pl.when(pl.program_id(0) == pl.num_programs(0) - 1)
    def _():
        each = jnp.zeros((8, 128), F32)
        for ref in (hca_ref, hda_ref, sc_ref):
            each = peak(each, ref[...])
        heads = jnp.zeros((8, 128), F32)
        for ref, most in ((hc_ref, X_TOP), (hd_ref, SLOPE_TOP)):
            heads = jnp.maximum(heads, most * peak(jnp.zeros((8, 128), F32), ref[...]))
        products = jnp.max(jnp.max(heads, axis=1, keepdims=True), axis=0, keepdims=True) * (
            X_TOP * tiles * TILE * pl.num_programs(0)
        )
        products = products * jnp.maximum(top_ref[:, 0:128], top_ref[:, 128:256])
        expo_ref[...] = exponents(jnp.maximum(each * 128.0, products))


ORDER = {
    2: [
        ("x", 0), ("x", 1), ("w", 0), ("f", 0), ("f", 1), ("l", 0), ("w", 1), ("l", 1),
        ("g", 0), ("b", 0), ("g", 1), ("b", 1), ("o", 0), ("o", 1),
    ],
}


TILES = 2


def layers(chunks, dense_values, dense_present, labels, weights, columns, emb, scale):
    fields = sum(c.shape[0] for c in chunks)
    dense, examples = dense_values.shape
    rows, hidden = columns[0].shape[0], columns[1].shape[0]
    tall = ceil_to(rows, 16)
    take = TILES * TILE
    column = lambda r: pl.BlockSpec((r, take), lambda t: (0, t))
    whole = lambda a: pl.BlockSpec(a.shape, lambda t: (0,) * a.ndim, pipeline_mode=pl.Buffered(1))
    kept = lambda r: pl.BlockSpec((r, 128), lambda t: (0, 0))
    shape = jax.ShapeDtypeStruct
    return pl.pallas_call(
        lambda *refs: layers_kernel((fields, emb, dense, len(chunks), TILES), scale, *refs),
        grid=(examples // take,),
        in_specs=[pl.BlockSpec((c.shape[0], PAD, take), lambda t: (0, 0, t)) for c in chunks]
        + [column(dense), column(dense), column(1)]
        + [pl.BlockSpec(memory_space=pltpu.HBM) for _ in weights]
        + [whole(a) for a in columns],
        out_specs=[
            column(1),
            column(tall),
            column(hidden + tall),
            pl.BlockSpec((fields, PAD, take), lambda t: (0, 0, t)),
            column(dense),
            kept(rows),
            kept(hidden),
            kept(8),
            kept(8),
        ],
        out_shape=[
            shape((1, examples), F32),
            shape((tall, examples), BF16),
            shape((hidden + tall, examples), BF16),
            shape((fields, PAD, examples), BF16),
            shape((dense, examples), F32),
            shape((rows, 128), F32),
            shape((hidden, 128), F32),
            shape((8, 128), F32),
            shape((8, 128), F32),
        ],
        scratch_shapes=[pltpu.VMEM((8, TILE), F32)]
        + [pltpu.VMEM(w.shape, BF16) for w in weights]
        + [pltpu.SemaphoreType.DMA((2,))]
        + [
            pltpu.VMEM((tall, TILE), F32),
            pltpu.VMEM((rows + hidden, TILE), F32),
            pltpu.VMEM((hidden, TILE), F32),
            pltpu.VMEM((hidden, TILE), F32),
        ]
        * TILES,
        compiler_params=params(40),
        cost_estimate=cost(2 * examples * rows * (2 * rows + 2 * hidden), 9 * 2**20 + 20 * rows * examples),
        name="layers",
    )(*chunks, dense_values, dense_present, labels, *map(in_hbm, weights), *columns)


def weight_kernel(rows, examples_all, half_ref, *refs):
    if len(refs) == 7:
        xa_ref, dd_ref, dc_ref, sc_ref, expo_ref, over, out_ref = refs
    else:
        xa_ref, dd_ref, dc_ref, sc_ref, expo_ref, tail_ref, hc_ref, hd_ref, out_ref, over = refs
    quarter = out_ref.shape[2] - FRONT
    half, j = half_ref[0], pl.program_id(0)
    first = half * pl.num_programs(0) + j == 0
    x = xa_ref[0:rows, :]
    hidden = over.shape[1] - 128
    if len(refs) > 7:

        @pl.when(j == 0)
        def _():
            tail = dot_nt(x, tail_ref[...])
            tail = jnp.concatenate([tail, jnp.zeros((rows, 128 - 16), F32)], axis=1)
            for r in range(0, hidden, 128):
                over[0:8, r : r + 128] = tail[r : r + 128].T[0:8]
            last = jnp.concatenate([tail[hidden:rows], jnp.zeros((128 - rows + hidden, 128), F32)], axis=0)
            over[0:8, hidden:] = last.T[0:8]
            over[8:, :] = jnp.zeros((8, hidden + 128), F32)
            for r in range(0, hidden, 128):
                for row, ref in ((8, hc_ref), (9, hd_ref)):
                    over[row : row + 1, r : r + 128] = jnp.sum(ref[r : r + 128, :].T, axis=0, keepdims=True)
            last = jnp.concatenate([hc_ref[hidden:rows, :], jnp.zeros((128 - rows + hidden, 128), F32)], axis=0)
            over[8:9, hidden:] = jnp.sum(last.T, axis=0, keepdims=True)

    deep = dot_nt(x, dd_ref[...])
    cross = dot_nt(x, dc_ref[...])
    at = pl.multiple_of((half * pl.num_programs(0) + j) * TILE, TILE)
    row = lax.broadcasted_iota(jnp.int32, (8, TILE), 0)
    heads = over[8:, pl.ds(at, TILE)]
    zeros = lambda n, m: jnp.zeros((n, m), F32)
    corner = jnp.concatenate([over[0:3, hidden:], zeros(3, TILE - 128)], axis=1)
    small = jnp.concatenate([zeros(2, TILE), corner, zeros(3, TILE)], axis=0)
    ends = jnp.concatenate([over[8:9, hidden:], zeros(1, TILE - 128)], axis=1)
    sums = jnp.sum(sc_ref[...], axis=1, keepdims=True)
    lane = lax.broadcasted_iota(jnp.int32, (8, TILE), 1)
    scalars = jnp.where(lane == 0, sums[0:1] / examples_all, jnp.where(lane == 1, sums[1:2], 0.0))
    small = small + jnp.where(row == 5, ends, 0.0) + jnp.where(row == 6, scalars, 0.0)
    heads = heads + jnp.where(first, small, 0.0)
    parts = [(0, deep), (rows, cross), (2 * rows, over[0:8, pl.ds(at, TILE)]), (2 * rows + 8, heads)]
    for q in range(4):
        for h in range(2):
            out_ref[q, h, 0:FRONT, :] = expo_ref[...]
    for base, part in parts:
        at = 0
        while at < part.shape[0]:
            q, r = divmod(base + at, quarter)
            n = min(part.shape[0] - at, quarter - r)
            place = jnp.where(half == 0, (0, 2, 1, 3)[q], q)
            for h in range(2):
                out_ref[place, h, FRONT + r : FRONT + r + n, :] = part[at : at + n, h * 128 : (h + 1) * 128]
            at += n


def weight_grads(half, xa, grads, hca, hda, sc, expo, examples_all, over=None):
    tall, examples = xa.shape
    rows, hidden = hca.shape[0], hda.shape[0]
    quarter = ceil_to(2 * rows + 16, 32) // 4
    steps = hidden // TILE // 2
    whole = lambda a: pl.BlockSpec(a.shape, lambda j, h: (0, 0), pipeline_mode=pl.Buffered(1))
    over_shape = jax.ShapeDtypeStruct((16, hidden + 128), F32)
    if over is None:
        more = (in_hbm(grads), hca, hda)
        more_specs = [pl.BlockSpec((16, examples), lambda j, h: (2 * hidden // 16, 0)), whole(hca), whole(hda)]
    else:
        more, more_specs = (over,), [whole(over)]
    return pl.pallas_call(
        lambda *refs: weight_kernel(rows, examples_all, *refs),
        grid_spec=pltpu.PrefetchScalarGridSpec(
            num_scalar_prefetch=1,
            grid=(steps,),
            in_specs=[
                whole(xa),
                pl.BlockSpec((TILE, examples), lambda j, h: (h[0] * steps + j, 0)),
                pl.BlockSpec((TILE, examples), lambda j, h: (2 * steps + h[0] * steps + j, 0)),
                whole(sc),
                whole(expo),
                *more_specs,
            ],
            out_specs=[pl.BlockSpec((4, 2, FRONT + quarter, 128), lambda j, h: (0, j, 0, 0))]
            + [pl.BlockSpec(over_shape.shape, lambda j, h: (0, 0))] * (over is None),
        ),
        out_shape=[jax.ShapeDtypeStruct((4, 2 * steps, FRONT + quarter, 128), F32)] + [over_shape] * (over is None),
        compiler_params=params(16),
        cost_estimate=cost(2 * examples * rows * hidden, 10 * rows * hidden),
        name="weight_grads",
    )(half.reshape(1).astype(jnp.int32), xa, in_hbm(grads), in_hbm(grads), sc, expo, *more)


def spread_kernel(first, core_ref, place_ref, block_ref, own_ref, sib_ref, *refs):
    out_ref, expo_ref, top_ref = refs[-3:]
    count, _, examples = own_ref.shape
    n_blocks = out_ref.shape[0] * out_ref.shape[1]

    @pl.when(pl.program_id(0) == 0)
    def _():
        top_ref[...] = jnp.zeros_like(top_ref)

    core = core_ref[0]
    every = []
    for k in range(count):
        f = first + pl.program_id(0) * count + k
        sums = jnp.zeros((n_blocks * PAD, HI), F32)
        for s, ref in enumerate((own_ref, sib_ref)):
            base = (core if s == 0 else 1 - core) * examples
            for at in range(0, examples, WIDE):
                cols = pl.ds(pl.multiple_of(base + at, WIDE), WIDE)
                place = place_ref[pl.ds(f, 1), cols]
                block = block_ref[pl.ds(f, 1), cols]
                grads = ref[k, :, at : at + WIDE].astype(F32)
                chosen = [jnp.where(block == b, grads, 0.0) for b in range(n_blocks)]
                chosen = jnp.concatenate(chosen, axis=0).astype(BF16)
                sums = sums + dot_nt(chosen, onehot_rows(place, WIDE))
        every.append(sums)
    for k, sums in enumerate(every):
        top_ref[...] = peak(top_ref[...], sums)
        for b in range(n_blocks):
            for h in range(2):
                out_ref[b // out_ref.shape[1], b % out_ref.shape[1], h, k * PAD : (k + 1) * PAD] = sums[
                    b * PAD : (b + 1) * PAD, h * 128 : (h + 1) * 128
                ]

    @pl.when(pl.program_id(0) == pl.num_programs(0) - 1)
    def _():
        expo_ref[...] = exponents(jnp.maximum(top_ref[:, 0:128], top_ref[:, 128:256]))


def spread(core, place, block, own, sib, span, part, blocks, into=None):
    fields, _, examples = own.shape
    count = span[1] - span[0]
    whole = lambda a: pl.BlockSpec(a.shape, lambda f: (0, 0), pipeline_mode=pl.Buffered(1))
    take = 2
    before = (part[0] - span[0]) // take
    more = [] if into is None else [into]
    return pl.pallas_call(
        lambda *refs: spread_kernel(part[0], *refs),
        grid=((part[1] - part[0]) // take,),
        in_specs=[pl.BlockSpec(memory_space=pltpu.SMEM), whole(place), whole(block)]
        + [pl.BlockSpec((take, PAD, examples), lambda f: (f + part[0] // take, 0, 0))] * 2
        + [pl.BlockSpec(memory_space=pl.ANY)] * len(more),
        out_specs=[
            pl.BlockSpec((2, blocks, 2, take * PAD, 128), lambda f: (0, 0, 0, f + before, 0)),
            pl.BlockSpec((8, 128), lambda f: (0, 0)),
        ],
        out_shape=[
            jax.ShapeDtypeStruct((2, blocks, 2, count * PAD, 128), F32),
            jax.ShapeDtypeStruct((8, 128), F32),
        ],
        input_output_aliases={5: 0} if more else {},
        scratch_shapes=[pltpu.VMEM((8, HI), F32)],
        compiler_params=params(10),
        cost_estimate=cost(8 * count * blocks * PAD * HI * examples, 4 * count * PAD * 16 * 128 * blocks),
        name="spread",
    )(core.reshape(1).astype(jnp.int32), place, block, own, sib, *more)


def flip(array, axis, bit):
    size = lax.axis_size(axis)
    return lax.ppermute(array, axis, [(i, i ^ (1 << bit)) for i in range(size)])


def bit_of(axis, bit):
    return (lax.axis_index(axis) >> bit) & 1


def crossed_pairs(stage, n_dp, n_mp):
    pairs = []
    for d in range(n_dp):
        for m in range(n_mp):
            along_dp = (m & 1) == stage
            to = (d ^ 1, m) if along_dp else (d, m ^ 2)
            pairs.append((d * n_mp + m, to[0] * n_mp + to[1]))
    return pairs


def crossed_flip(array, stage):
    return lax.ppermute(array, ("dp", "mp"), crossed_pairs(stage, lax.axis_size("dp"), lax.axis_size("mp")))


def crossed_bit(stage):
    return jnp.where(bit_of("mp", 0) == stage, bit_of("dp", 0), bit_of("mp", 1))


def after(value, token):
    return lax.optimization_barrier((value, token))[0]


def encode(values, expo, at):
    row = lax.broadcasted_iota(jnp.int32, values.shape, values.ndim - 2)
    here = expo.reshape((1,) * (values.ndim - 1) + (128,))
    return jnp.where(row == at, here, values * jnp.exp2(-here)).astype(F16)


def add(kept, expo, got, at):
    theirs = got[(0,) * (got.ndim - 2) + (at,)].astype(F32)
    total = kept + got.astype(F32) * jnp.exp2(theirs).reshape((1,) * (got.ndim - 1) + (128,))
    return total, jnp.maximum(expo, theirs) + 1.0


def block_of(acc, *index):
    start = (*index, *(0,) * (acc.ndim - len(index)))
    block = lax.dynamic_slice(acc, start, (1,) * len(index) + acc.shape[len(index) :])
    return block.reshape(acc.shape[len(index) :])


def decode(got, at):
    theirs = got[(0,) * (got.ndim - 2) + (at,)].astype(F32)
    return got.astype(F32) * jnp.exp2(theirs).reshape((1,) * (got.ndim - 1) + (128,)), theirs


def reduction(acc, expo, at, z_dim):
    (first, send_first), (second, send_second), *rest = stages()
    ahead = encode(block_of(acc, 1 - first, 1 - second), expo, at)
    got_ahead = send_first(ahead)
    behind = encode(block_of(acc, 1 - first, second), expo, at)
    got_behind = send_first(behind)
    token = yield ahead, behind
    more, theirs = decode(after(got_ahead, token), at)
    expo = jnp.maximum(expo, theirs) + 1.0
    message = encode(block_of(acc, first, 1 - second) + more, expo, at)
    got = send_second(message)
    token = yield message
    got, got_behind = after((got, got_behind), token)
    more, theirs = decode(got, at)
    acc = block_of(acc, first, second) + decode(got_behind, at)[0] + more
    expo = jnp.maximum(expo, theirs) + 1.0
    acc = jnp.swapaxes(acc.reshape(2, 2, *acc.shape[z_dim:]), 0, 1)
    for mine, send in rest:
        message = encode(block_of(acc, 1 - mine), expo, at)
        got = send(message)
        token = yield message
        more, theirs = decode(after(got, token), at)
        acc, expo = block_of(acc, mine) + more, jnp.maximum(expo, theirs) + 1.0
    yield acc, expo


def gathering(piece, scale, core):
    (first, send_first), (second, send_second), *rest = stages()
    to_sibling = lambda a: flip(a, "mp", 0)
    wider = lambda a: a.astype(F32) * scale
    for mine, send in reversed(rest):
        other = send(piece)
        token = yield piece
        other = after(other, token)
        low = mine == 0
        piece = jnp.stack([jnp.where(low, piece, other), jnp.where(low, other, piece)], axis=0)
    by_second, by_first, sib = send_second(piece), send_first(piece), to_sibling(piece)
    every = [((core, first, second), wider(piece))]
    token = yield piece
    by_second = after(by_second, token)
    by_both, sib_second = send_first(by_second), to_sibling(by_second)
    by_first = after(by_first, by_second)
    sib_first = to_sibling(by_first)
    every.append(((core, first, 1 - second), wider(by_second)))
    every.append(((core, 1 - first, second), wider(by_first)))
    every.append(((1 - core, second, first), wider(after(sib, token))))
    token = yield [values for _, values in every]
    by_both = after(by_both, token)
    sib_both = to_sibling(by_both)
    every.append(((core, 1 - first, 1 - second), wider(by_both)))
    every.append(((1 - core, second, 1 - first), wider(sib_second)))
    every.append(((1 - core, 1 - second, first), wider(sib_first)))
    every.append(((1 - core, 1 - second, 1 - first), wider(sib_both)))
    yield every


def stages():
    return [
        (crossed_bit(0), lambda a: crossed_flip(a, 0)),
        (crossed_bit(1), lambda a: crossed_flip(a, 1)),
        (bit_of("dp", 1), lambda a: flip(a, "dp", 1)),
        (bit_of("dp", 2), lambda a: flip(a, "dp", 2)),
    ]


def assemble_kernel(rows, full, at_ref, *refs):
    pieces, (cross_ref, deep_ref, vec_ref) = refs[:8], refs[8:]
    hidden = deep_ref.shape[1]
    extra = full - hidden
    quarter = pieces[0].shape[2] - FRONT
    kinds = [
        (0, full, deep_ref, 0),
        (full, full + 1, vec_ref, 9),
        (rows, rows + full, cross_ref, 0),
        (rows + full, rows + full + 1, vec_ref, 8),
        (2 * rows + 8, 2 * rows + 16, vec_ref, 0),
    ]

    def turned(lines):
        lines = jnp.concatenate([lines, jnp.zeros((128 - lines.shape[0], 128), F32)], axis=0)
        return lines.T

    def copy(piece, q, core):
        for z in range(4):
            block = piece.at[z % 2, z // 2]
            lanes = pl.ds(pl.multiple_of((core * 4 + z) * 128, 128), 128)
            for first, end, out, base in kinds:
                lo, hi = max(first, q * quarter), min(end, (q + 1) * quarter)
                if lo < hi:
                    place = slice(base + lo - first, base + hi - first)
                    out[place, lanes] = block[FRONT + lo - q * quarter : FRONT + hi - q * quarter, :]
            if q == 3:
                over = FRONT + 2 * rows - q * quarter
                cross_ref[lanes, hidden:full] = turned(block[over : over + 8, :])[:, 0:extra]
                if z == 0:

                    @pl.when(core == 0)
                    def _():
                        corner = turned(block[over + 10 : over + 10 + extra, :])
                        cross_ref[hidden:full, hidden:full] = corner[0:extra, 0:extra]
                        vec_ref[8:9, hidden:full] = corner[extra : extra + 1, 0:extra]
                        vec_ref[0:1, hidden:full] = block[over + 13 : over + 14, 0:extra]

    for k, piece in enumerate(pieces):
        for q in range(4):
            pl.when(at_ref[k] == q)(lambda piece=piece, q=q, k=k: copy(piece, q, at_ref[8 + k]))


def assemble(pieces, rows, full, hidden):
    quarters = [jnp.where(c == 0, s * 2 + f, f * 2 + s) for (c, f, s), _ in pieces]
    at = jnp.stack([jnp.asarray(v, jnp.int32) for v in quarters + [c for (c, _, _), _ in pieces]])
    shape = jax.ShapeDtypeStruct
    return pl.pallas_call(
        lambda *refs: assemble_kernel(rows, full, *refs),
        in_specs=[pl.BlockSpec(memory_space=pltpu.SMEM)] + [pl.BlockSpec(memory_space=pltpu.VMEM)] * 8,
        out_shape=[shape((full, full), F32), shape((full, hidden), F32), shape((16, hidden + 128), F32)],
        compiler_params=params(14),
        cost_estimate=cost(0, 16 * rows * hidden),
        name="assemble",
    )(at, *[values for _, values in pieces])


def table_place(ids, table_rows, n_dp, core):
    upper = ids // (2 * table_rows)
    rest = ids % table_rows
    if n_dp == 8:
        piece = table_rows // n_dp
        at = rest // piece
        low = at % 2
        first = jnp.where(core == 0, low, upper)
        second = jnp.where(core == 0, upper, low)
        block = first * 4 + second * 2 + at // 4
        place = (at // 2) % 2 * piece + rest % piece
    else:
        block = upper * (table_rows // HI) + rest // HI
        place = rest % HI
    return place, jnp.where((ids // table_rows) % 2 == core, block, -1)


def body(
    field_ids,
    field_present,
    dense_values,
    dense_present,
    clicked,
    tables,
    cross_weight,
    cross_bias,
    deep_weight,
    deep_bias,
    head_cross,
    head_deep,
    head_bias,
):
    fields, batch_group = field_ids.shape
    table_rows, cat = tables.shape
    emb = cat // fields
    full, hidden = deep_weight.shape
    dense = full - cat
    n_dp, n_mp = lax.axis_size("dp"), lax.axis_size("mp")
    examples = batch_group // n_mp
    examples_all = batch_group * n_dp
    blocks = table_rows // HI
    rows = ceil_to(full + ONES, 8)
    me = lax.axis_index("mp")
    core = me & 1

    chosen = jnp.where(field_present > 0, field_ids, 0)
    own_ids = lax.dynamic_slice_in_dim(chosen, me * examples, examples, 1)
    place_own = own_ids & (HI - 1)
    block_own = (own_ids // HI) ^ (me * blocks)
    pair_ids = lax.dynamic_slice_in_dim(chosen, (me - core) * examples, 2 * examples, 1)
    place, block = table_place(pair_ids, table_rows, n_dp, core)

    columns = tables.T
    cuts = [(0, CUTS[0]), CUTS, (CUTS[1], fields)]
    far = [columns[a * emb : b * emb] for a, b in cuts[:2]]
    first_weight = after(cross_weight, far)
    weights = prepare(first_weight, deep_weight, cross_bias, deep_bias, head_cross, head_deep, rows)
    far.append(after(columns, weights[0])[cuts[2][0] * emb :])
    far = [flip(part, "mp", 1) for part in far]
    near = flip(columns, "mp", 0)
    place, block = after((place, block), weights[0])
    token = place, block
    found = []
    for k, (a, b) in enumerate(cuts):
        far_near = flip(after(far[k], token), "mp", 0)
        found.append(lookup(place_own[a:b], block_own[a:b], (columns, near, far[k], far_near), a * emb, emb))
        token = found[-1]

    logit, xa, grads, demb, dense_grad, hca, hda, sc, expo = layers(
        found,
        dense_values,
        dense_present,
        clicked[None, :],
        weights[:2],
        (*weights[2:], jnp.broadcast_to(head_bias[:, None], (8, 128))),
        emb,
        1.0 / math.sqrt(examples_all),
    )
    demb_sib = flip(demb, "mp", 0)
    grad_args = (xa, grads, hca, hda, sc, expo, examples_all)
    away, over = weight_grads(1 - core, *grad_args)
    if n_dp == 8:
        away = encode(away, expo[0], FRONT - 1)
    got = flip(away, "mp", 0)
    (sums,) = weight_grads(after(core, away), *grad_args, over)
    spans = [(0, 12), (12, fields)]

    def table_part(token, span, part, into=None):
        given = after(demb, token)
        values, top = spread(core, place, block, given, demb_sib, span, part, blocks, None if into is None else into[0])
        top = top[0] if into is None else jnp.maximum(top[0], into[1])
        return values, top

    if n_dp == 8:
        got = after(got, sums)
        both, expo = add(sums, expo[0], got, FRONT - 1)
        both = both.reshape(2, 2, *sums.shape[1:])
        weight_chain = reduction(both, expo, FRONT - 1, 1)
        token = next(weight_chain)
        table_chains = []
        for span in spans:
            part, top = table_part(token, span, span)
            part = part.reshape(2, 2, 2, 2, *part.shape[3:])
            table_chains.append(reduction(part, top, PAD - 1, 2))
            token = weight_chain.send(part)
            token = token, next(table_chains[-1])
        chain = {"w": weight_chain, "a": table_chains[0], "b": table_chains[1]}
        table_out, total = {}, None
        for name in "awbawwabwabwbw":
            token = chain[name].send(token)
            if name == "w" and total is None and isinstance(token, tuple):
                total, expo = token
                total = (total * jnp.exp2(-expo)[None, :]).astype(F16)
                chain["w"] = gathering(total, jnp.exp2(expo), core)
                token = next(chain["w"])
            elif name != "w" and isinstance(token, tuple):
                table_out[name] = token[0]
                if len(table_out) == 2:
                    tables_grad = jnp.concatenate([table_out["a"], table_out["b"]], axis=0)
                    token = tables_grad = tables_grad.reshape(fields, PAD, -1)[:, :emb].reshape(cat, -1)
                else:
                    token = token[0]
        pieces = token
    else:
        summed = lax.psum(sums + got, "dp")
        summed = summed + flip(summed, "mp", 1)
        pieces = lax.all_gather(summed, "mp")[0:2].reshape(2, 2, 2, 2, 2, *sums.shape[2:])
        pieces = jnp.swapaxes(pieces, 3, 4)
        pieces = [((c, f, s), pieces[c, f, s]) for c in range(2) for f in range(2) for s in range(2)]
        table_out = jnp.concatenate([table_part(sums, span, span)[0] for span in spans], axis=3)
        table_out = table_out.transpose(0, 3, 1, 2, 4).reshape(2, fields * PAD, table_rows)
        upper = bit_of("mp", 1)
        away = lax.dynamic_index_in_dim(table_out, 1 - upper, 0, keepdims=False)
        table_out = lax.dynamic_index_in_dim(table_out, upper, 0, keepdims=False) + flip(away, "mp", 1)
        table_out = lax.psum_scatter(table_out, "dp", scatter_dimension=1, tiled=True)
        tables_grad = table_out.reshape(fields, PAD, -1)[:, :emb].reshape(cat, -1)
    cross_grad, deep_grad, small = assemble(pieces, rows, full, hidden)
    return (
        logit[0],
        small[6, 0],
        dense_grad,
        tables_grad.T,
        cross_grad,
        small[8, 0:full],
        deep_grad,
        small[9, 0:hidden],
        small[0, 0:full],
        small[1, 0:hidden],
        small[6, 1:2],
    )


def solution(mesh):
    placed = (
        P(None, "dp"),
        P(None, "dp"),
        P(None, ("dp", "mp")),
        P(None, ("dp", "mp")),
        P(("dp", "mp")),
        P("mp", None),
        P(),
        P(),
        P(),
        P(),
        P(),
        P(),
        P(),
    )
    return jax.shard_map(
        body,
        mesh=mesh,
        in_specs=placed,
        out_specs=(
            P(("dp", "mp")),
            P(),
            P(None, ("dp", "mp")),
            P(("mp", "dp"), None),
            P(),
            P(),
            P(),
            P(),
            P(),
            P(),
            P(),
        ),
        check_vma=False,
    )
```

```python
import math

import jax
import jax.numpy as jnp
from jax import lax
from jax.experimental import pallas as pl
from jax.experimental.pallas import tpu as pltpu
from jax.sharding import PartitionSpec as P

BF16, F32, F16 = jnp.bfloat16, jnp.float32, jnp.float16
HI = 256
ONES = 3
SLOPE_TOP = 1.25
X_TOP = 6.0
FRONT = 8
PAD = 40
TILE = 256
CUTS = (13, 22)
WIDE = 512
GELU_S = math.sqrt(2.0 / math.pi)
GELU_C = 0.044715


def params(mebibytes):
    return pltpu.CompilerParams(vmem_limit_bytes=mebibytes * 1024 * 1024)


def cost(flops, moved):
    return pl.CostEstimate(flops=int(flops), bytes_accessed=int(moved), transcendentals=0)


def in_hbm(array):
    return pltpu.with_memory_space_constraint(array, pltpu.HBM)


def in_vmem(array):
    return pltpu.with_memory_space_constraint(array, pltpu.VMEM)


def ceil_to(value, unit):
    return -(-value // unit) * unit


def dot_nn(left, right):
    return jnp.dot(left, right, preferred_element_type=F32)


def dot_nt(left, right, precision=None):
    return lax.dot_general(
        left, right, (((1,), (1,)), ((), ())), preferred_element_type=F32, precision=precision
    )


def onehot_rows(place, width):
    rows = lax.broadcasted_iota(jnp.int16, (HI, width), 0)
    return jnp.where(rows == place.astype(jnp.int16), jnp.ones((), BF16), jnp.zeros((), BF16))


def prepare_kernel(cw_ref, dw_ref, cb_ref, db_ref, hc_ref, hd_ref, ww_ref, wb_ref, hco_ref, hdo_ref, pad):
    full, hidden = dw_ref.shape
    rows = wb_ref.shape[0]
    pad[...] = jnp.zeros_like(pad)
    for source, bias, more, base, width in ((dw_ref, db_ref, 0.0, 0, hidden), (cw_ref, cb_ref, 1.0, hidden, full)):
        pad[0:full, 0:width] = source[...].astype(F32)
        rest = bias[:, 0:width] + more
        for k in range(ONES):
            part = rest.astype(BF16).astype(F32)
            pad[full + k : full + k + 1, 0:width] = part
            rest = rest - part
        if width < rows:
            pad[:, width:] = jnp.zeros((pad.shape[0], pad.shape[1] - width), F32)
        wide_width = hidden if base == 0 else rows
        wb_ref[:, base : base + wide_width] = pad[0:rows, 0:wide_width].astype(BF16)
        for r in range(0, wide_width, 128):
            n = min(128, wide_width - r)
            turned = pad[:, r : r + 128].T
            ww_ref[base + r : base + r + n, :] = turned[0:n, 0:rows].astype(BF16)
    for source, out in ((hc_ref, hco_ref), (hd_ref, hdo_ref)):
        for r in range(0, out.shape[0], 128):
            n = min(128, out.shape[0] - r)
            line = source[:, r : r + 128]
            out[r : r + n, :] = jnp.broadcast_to(line, (128, 128)).T[0:n]


def prepare(cross_weight, deep_weight, cross_bias, deep_bias, head_cross, head_deep, rows):
    full, hidden = deep_weight.shape
    wide_rows = ceil_to(rows, 128)
    line = lambda v: jnp.pad(v, (0, ceil_to(v.shape[0], 128) - v.shape[0]))[None, :]
    shape = jax.ShapeDtypeStruct
    return pl.pallas_call(
        prepare_kernel,
        out_shape=[
            shape((hidden + rows, rows), BF16),
            shape((rows, hidden + rows), BF16),
            shape((rows, 128), F32),
            shape((hidden, 128), F32),
        ],
        scratch_shapes=[pltpu.VMEM((wide_rows, wide_rows), F32)],
        compiler_params=params(16),
        cost_estimate=cost(0, 16 * rows * rows),
        name="prepare",
    )(cross_weight, deep_weight, line(cross_bias), line(deep_bias), line(head_cross), line(head_deep))


def lookup_kernel(emb, blocks, at_row, place_ref, block_ref, *refs):
    sources, out_ref, flat, packed = refs[0:4], refs[4], refs[5], refs[6]
    n_fields, examples = place_ref.shape
    rows = emb * n_fields
    for s, source in enumerate(sources):
        first = at_row if s < 2 else 0
        flat[s, 0:rows, :] = source[first : first + rows, :].astype(F32)
    for f in range(n_fields):
        for s in range(4):
            for b in range(blocks):
                piece = flat[s, emb * f : emb * f + PAD, b * HI : (b + 1) * HI]
                at = (s * blocks + b) * PAD
                packed[f, at : at + PAD, :] = piece.astype(BF16)

    for f in range(n_fields):
        block = block_ref[f : f + 1, :]
        found = dot_nn(packed[f], onehot_rows(place_ref[f : f + 1, :], examples))
        acc = found[0:PAD]
        for b in range(1, 4 * blocks):
            acc = jnp.where(block == b, found[b * PAD : (b + 1) * PAD], acc)
        out_ref[f] = acc.astype(BF16)


def lookup(place, block, sources, at_row, emb):
    n_fields, examples = place.shape
    width = sources[0].shape[1]
    blocks = width // HI
    n_rows = 4 * blocks * PAD
    return pl.pallas_call(
        lambda *refs: lookup_kernel(emb, blocks, at_row, *refs),
        out_shape=jax.ShapeDtypeStruct((n_fields, PAD, examples), BF16),
        scratch_shapes=[
            pltpu.VMEM((4, ceil_to(n_fields * emb, 8) + 8, width), F32),
            pltpu.VMEM((n_fields, n_rows, HI), BF16),
        ],
        compiler_params=params(16),
        cost_estimate=cost(2 * n_fields * n_rows * HI * examples, 4 * n_fields * PAD * examples),
        name="lookup",
    )(place, block, *sources)


def wide(column, width):
    return jnp.concatenate([column] * (width // 128), axis=1)


def fold(values):
    total = values[:, 0:128]
    for at in range(128, values.shape[1], 128):
        total = total + values[:, at : at + 128]
    return total


def peak(top, values):
    for r in range(0, values.shape[0], 8):
        top = jnp.maximum(top, jnp.abs(values[r : r + 8]))
    return top


def exponents(top):
    most = jnp.max(jnp.max(top, axis=1, keepdims=True), axis=0, keepdims=True)
    return jnp.broadcast_to(jnp.ceil(jnp.log(jnp.maximum(most, 1e-30)) * (1.0 / math.log(2.0))) - 14.0, (8, 128))


def layers_kernel(sizes, scale, *refs):
    fields, emb, dense, n_chunks, tiles = sizes
    chunks = refs[:n_chunks]
    (dv_ref, dm_ref, lab_ref, ww_ref, wb_ref, hc_ref, hd_ref, hb_ref) = refs[n_chunks : n_chunks + 8]
    (logit_ref, xa_ref, grad_ref, demb_ref, dg_ref, hca_ref, hda_ref, sc_ref, expo_ref) = refs[
        n_chunks + 8 : n_chunks + 17
    ]
    top_ref, wws_ref, wbs_ref, sems, *scratch = refs[n_chunks + 17 :]
    loads = [
        pltpu.make_async_copy(ww_ref, wws_ref, sems.at[0]),
        pltpu.make_async_copy(wb_ref, wbs_ref, sems.at[1]),
    ]
    start = pl.program_id(0) == 0
    hidden = hda_ref.shape[0]
    rows = hca_ref.shape[0]
    width = TILE
    cat = fields * emb
    full = cat + dense
    step = 128
    cuts = [(a, min(a + step, rows)) for a in range(0, rows, step)]
    hid_cuts = [(a, min(a + step, hidden)) for a in range(0, hidden, step)]
    cols = [slice(k * TILE, (k + 1) * TILE) for k in range(tiles)]
    tall = xa_ref.shape[0]

    @pl.when(start)
    def _():
        for load in loads:
            load.start()
        hca_ref[...] = jnp.zeros_like(hca_ref)
        hda_ref[...] = jnp.zeros_like(hda_ref)
        sc_ref[...] = jnp.zeros_like(sc_ref)
        top_ref[...] = jnp.zeros_like(top_ref)

    def gather(k):
        x_ref = scratch[4 * k]
        f = 0
        for chunk in chunks:
            for c in range(chunk.shape[0]):
                x_ref[emb * f : emb * f + PAD, :] = chunk[c, :, cols[k]].astype(F32)
                f += 1
        x_ref[cat:full, :] = dv_ref[:, cols[k]] * dm_ref[:, cols[k]].astype(F32)
        x_ref[full:tall, :] = (
            lax.broadcasted_iota(jnp.int32, (tall - full, width), 0) < ONES
        ).astype(F32)
        xa_ref[:, cols[k]] = x_ref[0:tall, :].astype(BF16)

    def forward(k):
        scratch[4 * k + 1][...] = dot_nn(wws_ref[...], xa_ref[0:rows, cols[k]])

    def logits(k):
        x_ref, pre_ref, act_ref, slope_ref = scratch[4 * k : 4 * k + 4]
        total = jnp.zeros((8, width), F32)
        for a, b in cuts:
            cp = pre_ref[hidden + a : hidden + b, :]
            term = (x_ref[a:b, :] * cp) * wide(hc_ref[a:b, :], width)
            for r in range(0, b - a, 8):
                total = total + term[r : r + 8]
        for a, b in hid_cuts:
            v = pre_ref[a:b, :]
            vv = v * v
            half = 0.5 + 0.5 * jnp.tanh(v * (GELU_S + (GELU_S * GELU_C) * vv))
            act = v * half
            act_ref[a:b, :] = act
            slope_ref[a:b, :] = half + (act * (1.0 - half)) * ((2.0 * GELU_S) + (6.0 * GELU_S * GELU_C) * vv)
            term = act * wide(hd_ref[a:b, :], width)
            for r in range(0, b - a, 8):
                total = total + term[r : r + 8]
        logit = jnp.sum(total, axis=0, keepdims=True) + hb_ref[0:1, 0:1]
        logit_ref[:, cols[k]] = logit
        labels = lab_ref[:, cols[k]].astype(F32)
        small = jnp.exp(-jnp.abs(logit))
        loss = jnp.maximum(logit, 0.0) + jnp.log1p(small) - labels * logit
        sig = jnp.where(logit >= 0.0, 1.0, small) / (1.0 + small)
        dlogit = (sig - labels) * scale
        sc_ref[0:1, :] += fold(loss)
        sc_ref[1:2, :] += fold(dlogit)
        top_ref[...] = jnp.maximum(top_ref[...], jnp.abs(dlogit))
        return dlogit

    def gradients(k, dlogit):
        x_ref, pre_ref, act_ref, slope_ref = scratch[4 * k : 4 * k + 4]
        for a, b in hid_cuts:
            hda_ref[a:b, :] += fold(dlogit * act_ref[a:b, :])
            dd = (dlogit * wide(hd_ref[a:b, :], width)) * slope_ref[a:b, :]
            grad_ref[a:b, cols[k]] = dd.astype(BF16)
        for a, b in cuts:
            cp = pre_ref[hidden + a : hidden + b, :]
            dx = dlogit * x_ref[a:b, :]
            hc = wide(hc_ref[a:b, :], width)
            hca_ref[a:b, :] += fold(dx * cp)
            dc = dx * hc
            if b == rows:
                dc = jnp.concatenate([dc, jnp.zeros((tall - rows, width), F32)], axis=0)
            grad_ref[hidden + a : hidden + a + dc.shape[0], cols[k]] = dc.astype(BF16)
            pre_ref[hidden + a : hidden + b, :] = (dlogit * hc) * cp

    def backward(k):
        x_ref, pre_ref = scratch[4 * k], scratch[4 * k + 1]
        x_ref[0:rows, :] = pre_ref[hidden:, :] + dot_nn(wbs_ref[...], grad_ref[0 : hidden + rows, cols[k]])

    def give(k):
        x_ref = scratch[4 * k]
        for f in range(fields):
            demb_ref[f, :, cols[k]] = x_ref[emb * f : emb * f + PAD, :].astype(BF16)
        dg_ref[:, cols[k]] = x_ref[cat:full, :] * dm_ref[:, cols[k]].astype(F32)

    dlogits = {}
    for phase, k in ORDER[tiles]:
        if phase == "w":
            pl.when(start)(loads[k].wait)
        elif phase == "x":
            gather(k)
        elif phase == "f":
            forward(k)
        elif phase == "l":
            dlogits[k] = logits(k)
        elif phase == "g":
            gradients(k, dlogits[k])
        elif phase == "b":
            backward(k)
        else:
            give(k)

    @pl.when(pl.program_id(0) == pl.num_programs(0) - 1)
    def _():
        each = jnp.zeros((8, 128), F32)
        for ref in (hca_ref, hda_ref, sc_ref):
            each = peak(each, ref[...])
        heads = jnp.zeros((8, 128), F32)
        for ref, most in ((hc_ref, X_TOP), (hd_ref, SLOPE_TOP)):
            heads = jnp.maximum(heads, most * peak(jnp.zeros((8, 128), F32), ref[...]))
        products = jnp.max(jnp.max(heads, axis=1, keepdims=True), axis=0, keepdims=True) * (
            X_TOP * tiles * TILE * pl.num_programs(0)
        )
        products = products * jnp.maximum(top_ref[:, 0:128], top_ref[:, 128:256])
        expo_ref[...] = exponents(jnp.maximum(each * 128.0, products))


ORDER = {
    2: [
        ("x", 0), ("x", 1), ("w", 0), ("f", 0), ("f", 1), ("l", 0), ("w", 1), ("l", 1),
        ("g", 0), ("b", 0), ("g", 1), ("b", 1), ("o", 0), ("o", 1),
    ],
}


TILES = 2


def layers(chunks, dense_values, dense_present, labels, weights, columns, emb, scale):
    fields = sum(c.shape[0] for c in chunks)
    dense, examples = dense_values.shape
    rows, hidden = columns[0].shape[0], columns[1].shape[0]
    tall = ceil_to(rows, 16)
    take = TILES * TILE
    column = lambda r: pl.BlockSpec((r, take), lambda t: (0, t))
    whole = lambda a: pl.BlockSpec(a.shape, lambda t: (0,) * a.ndim, pipeline_mode=pl.Buffered(1))
    kept = lambda r: pl.BlockSpec((r, 128), lambda t: (0, 0))
    shape = jax.ShapeDtypeStruct
    return pl.pallas_call(
        lambda *refs: layers_kernel((fields, emb, dense, len(chunks), TILES), scale, *refs),
        grid=(examples // take,),
        in_specs=[pl.BlockSpec((c.shape[0], PAD, take), lambda t: (0, 0, t)) for c in chunks]
        + [column(dense), column(dense), column(1)]
        + [pl.BlockSpec(memory_space=pltpu.HBM) for _ in weights]
        + [whole(a) for a in columns],
        out_specs=[
            column(1),
            column(tall),
            column(hidden + tall),
            pl.BlockSpec((fields, PAD, take), lambda t: (0, 0, t)),
            column(dense),
            kept(rows),
            kept(hidden),
            kept(8),
            kept(8),
        ],
        out_shape=[
            shape((1, examples), F32),
            shape((tall, examples), BF16),
            shape((hidden + tall, examples), BF16),
            shape((fields, PAD, examples), BF16),
            shape((dense, examples), F32),
            shape((rows, 128), F32),
            shape((hidden, 128), F32),
            shape((8, 128), F32),
            shape((8, 128), F32),
        ],
        scratch_shapes=[pltpu.VMEM((8, TILE), F32)]
        + [pltpu.VMEM(w.shape, BF16) for w in weights]
        + [pltpu.SemaphoreType.DMA((2,))]
        + [
            pltpu.VMEM((tall, TILE), F32),
            pltpu.VMEM((rows + hidden, TILE), F32),
            pltpu.VMEM((hidden, TILE), F32),
            pltpu.VMEM((hidden, TILE), F32),
        ]
        * TILES,
        compiler_params=params(40),
        cost_estimate=cost(2 * examples * rows * (2 * rows + 2 * hidden), 9 * 2**20 + 20 * rows * examples),
        name="layers",
    )(*chunks, dense_values, dense_present, labels, *map(in_hbm, weights), *columns)


def weight_kernel(rows, examples_all, half_ref, *refs):
    if len(refs) == 7:
        xa_ref, dd_ref, dc_ref, sc_ref, expo_ref, over, out_ref = refs
    else:
        xa_ref, dd_ref, dc_ref, sc_ref, expo_ref, tail_ref, hc_ref, hd_ref, out_ref, over = refs
    quarter = out_ref.shape[2] - FRONT
    half, j = half_ref[0], pl.program_id(0)
    first = half * pl.num_programs(0) + j == 0
    x = xa_ref[0:rows, :]
    hidden = over.shape[1] - 128
    if len(refs) > 7:

        @pl.when(j == 0)
        def _():
            tail = dot_nt(x, tail_ref[...])
            tail = jnp.concatenate([tail, jnp.zeros((rows, 128 - 16), F32)], axis=1)
            for r in range(0, hidden, 128):
                over[0:8, r : r + 128] = tail[r : r + 128].T[0:8]
            last = jnp.concatenate([tail[hidden:rows], jnp.zeros((128 - rows + hidden, 128), F32)], axis=0)
            over[0:8, hidden:] = last.T[0:8]
            over[8:, :] = jnp.zeros((8, hidden + 128), F32)
            for r in range(0, hidden, 128):
                for row, ref in ((8, hc_ref), (9, hd_ref)):
                    over[row : row + 1, r : r + 128] = jnp.sum(ref[r : r + 128, :].T, axis=0, keepdims=True)
            last = jnp.concatenate([hc_ref[hidden:rows, :], jnp.zeros((128 - rows + hidden, 128), F32)], axis=0)
            over[8:9, hidden:] = jnp.sum(last.T, axis=0, keepdims=True)

    deep = dot_nt(x, dd_ref[...])
    cross = dot_nt(x, dc_ref[...])
    at = pl.multiple_of((half * pl.num_programs(0) + j) * TILE, TILE)
    row = lax.broadcasted_iota(jnp.int32, (8, TILE), 0)
    heads = over[8:, pl.ds(at, TILE)]
    zeros = lambda n, m: jnp.zeros((n, m), F32)
    corner = jnp.concatenate([over[0:3, hidden:], zeros(3, TILE - 128)], axis=1)
    small = jnp.concatenate([zeros(2, TILE), corner, zeros(3, TILE)], axis=0)
    ends = jnp.concatenate([over[8:9, hidden:], zeros(1, TILE - 128)], axis=1)
    sums = jnp.sum(sc_ref[...], axis=1, keepdims=True)
    lane = lax.broadcasted_iota(jnp.int32, (8, TILE), 1)
    scalars = jnp.where(lane == 0, sums[0:1] / examples_all, jnp.where(lane == 1, sums[1:2], 0.0))
    small = small + jnp.where(row == 5, ends, 0.0) + jnp.where(row == 6, scalars, 0.0)
    heads = heads + jnp.where(first, small, 0.0)
    parts = [(0, deep), (rows, cross), (2 * rows, over[0:8, pl.ds(at, TILE)]), (2 * rows + 8, heads)]
    for q in range(4):
        for h in range(2):
            out_ref[q, h, 0:FRONT, :] = expo_ref[...]
    for base, part in parts:
        at = 0
        while at < part.shape[0]:
            q, r = divmod(base + at, quarter)
            n = min(part.shape[0] - at, quarter - r)
            place = jnp.where(half == 0, (0, 2, 1, 3)[q], q)
            for h in range(2):
                out_ref[place, h, FRONT + r : FRONT + r + n, :] = part[at : at + n, h * 128 : (h + 1) * 128]
            at += n


def weight_grads(half, xa, grads, hca, hda, sc, expo, examples_all, over=None):
    tall, examples = xa.shape
    rows, hidden = hca.shape[0], hda.shape[0]
    quarter = ceil_to(2 * rows + 16, 32) // 4
    steps = hidden // TILE // 2
    whole = lambda a: pl.BlockSpec(a.shape, lambda j, h: (0, 0), pipeline_mode=pl.Buffered(1))
    over_shape = jax.ShapeDtypeStruct((16, hidden + 128), F32)
    if over is None:
        more = (in_hbm(grads), hca, hda)
        more_specs = [pl.BlockSpec((16, examples), lambda j, h: (2 * hidden // 16, 0)), whole(hca), whole(hda)]
    else:
        more, more_specs = (over,), [whole(over)]
    return pl.pallas_call(
        lambda *refs: weight_kernel(rows, examples_all, *refs),
        grid_spec=pltpu.PrefetchScalarGridSpec(
            num_scalar_prefetch=1,
            grid=(steps,),
            in_specs=[
                whole(xa),
                pl.BlockSpec((TILE, examples), lambda j, h: (h[0] * steps + j, 0)),
                pl.BlockSpec((TILE, examples), lambda j, h: (2 * steps + h[0] * steps + j, 0)),
                whole(sc),
                whole(expo),
                *more_specs,
            ],
            out_specs=[pl.BlockSpec((4, 2, FRONT + quarter, 128), lambda j, h: (0, j, 0, 0))]
            + [pl.BlockSpec(over_shape.shape, lambda j, h: (0, 0))] * (over is None),
        ),
        out_shape=[jax.ShapeDtypeStruct((4, 2 * steps, FRONT + quarter, 128), F32)] + [over_shape] * (over is None),
        compiler_params=params(16),
        cost_estimate=cost(2 * examples * rows * hidden, 10 * rows * hidden),
        name="weight_grads",
    )(half.reshape(1).astype(jnp.int32), xa, in_hbm(grads), in_hbm(grads), sc, expo, *more)


def spread_kernel(first, core_ref, place_ref, block_ref, own_ref, sib_ref, *refs):
    out_ref, expo_ref, top_ref = refs[-3:]
    count, _, examples = own_ref.shape
    n_blocks = out_ref.shape[0] * out_ref.shape[1]

    @pl.when(pl.program_id(0) == 0)
    def _():
        top_ref[...] = jnp.zeros_like(top_ref)

    core = core_ref[0]
    every = []
    for k in range(count):
        f = first + pl.program_id(0) * count + k
        sums = jnp.zeros((n_blocks * PAD, HI), F32)
        for s, ref in enumerate((own_ref, sib_ref)):
            base = (core if s == 0 else 1 - core) * examples
            for at in range(0, examples, WIDE):
                cols = pl.ds(pl.multiple_of(base + at, WIDE), WIDE)
                place = place_ref[pl.ds(f, 1), cols]
                block = block_ref[pl.ds(f, 1), cols]
                grads = ref[k, :, at : at + WIDE].astype(F32)
                chosen = [jnp.where(block == b, grads, 0.0) for b in range(n_blocks)]
                chosen = jnp.concatenate(chosen, axis=0).astype(BF16)
                sums = sums + dot_nt(chosen, onehot_rows(place, WIDE))
        every.append(sums)
    for k, sums in enumerate(every):
        top_ref[...] = peak(top_ref[...], sums)
        for b in range(n_blocks):
            for h in range(2):
                out_ref[b // out_ref.shape[1], b % out_ref.shape[1], h, k * PAD : (k + 1) * PAD] = sums[
                    b * PAD : (b + 1) * PAD, h * 128 : (h + 1) * 128
                ]

    @pl.when(pl.program_id(0) == pl.num_programs(0) - 1)
    def _():
        expo_ref[...] = exponents(jnp.maximum(top_ref[:, 0:128], top_ref[:, 128:256]))


def spread(core, place, block, own, sib, span, part, blocks, into=None):
    fields, _, examples = own.shape
    count = span[1] - span[0]
    whole = lambda a: pl.BlockSpec(a.shape, lambda f: (0, 0), pipeline_mode=pl.Buffered(1))
    take = 2
    before = (part[0] - span[0]) // take
    more = [] if into is None else [into]
    return pl.pallas_call(
        lambda *refs: spread_kernel(part[0], *refs),
        grid=((part[1] - part[0]) // take,),
        in_specs=[pl.BlockSpec(memory_space=pltpu.SMEM), whole(place), whole(block)]
        + [pl.BlockSpec((take, PAD, examples), lambda f: (f + part[0] // take, 0, 0))] * 2
        + [pl.BlockSpec(memory_space=pl.ANY)] * len(more),
        out_specs=[
            pl.BlockSpec((2, blocks, 2, take * PAD, 128), lambda f: (0, 0, 0, f + before, 0)),
            pl.BlockSpec((8, 128), lambda f: (0, 0)),
        ],
        out_shape=[
            jax.ShapeDtypeStruct((2, blocks, 2, count * PAD, 128), F32),
            jax.ShapeDtypeStruct((8, 128), F32),
        ],
        input_output_aliases={5: 0} if more else {},
        scratch_shapes=[pltpu.VMEM((8, HI), F32)],
        compiler_params=params(10),
        cost_estimate=cost(8 * count * blocks * PAD * HI * examples, 4 * count * PAD * 16 * 128 * blocks),
        name="spread",
    )(core.reshape(1).astype(jnp.int32), place, block, own, sib, *more)


def flip(array, axis, bit):
    size = lax.axis_size(axis)
    return lax.ppermute(array, axis, [(i, i ^ (1 << bit)) for i in range(size)])


def bit_of(axis, bit):
    return (lax.axis_index(axis) >> bit) & 1


def crossed_pairs(stage, n_dp, n_mp):
    pairs = []
    for d in range(n_dp):
        for m in range(n_mp):
            along_dp = (m & 1) == stage
            to = (d ^ 1, m) if along_dp else (d, m ^ 2)
            pairs.append((d * n_mp + m, to[0] * n_mp + to[1]))
    return pairs


def crossed_flip(array, stage):
    return lax.ppermute(array, ("dp", "mp"), crossed_pairs(stage, lax.axis_size("dp"), lax.axis_size("mp")))


def crossed_bit(stage):
    return jnp.where(bit_of("mp", 0) == stage, bit_of("dp", 0), bit_of("mp", 1))


def after(value, token):
    return lax.optimization_barrier((value, token))[0]


def encode(values, expo, at):
    row = lax.broadcasted_iota(jnp.int32, values.shape, values.ndim - 2)
    here = expo.reshape((1,) * (values.ndim - 1) + (128,))
    return jnp.where(row == at, here, values * jnp.exp2(-here)).astype(F16)


def add(kept, expo, got, at):
    theirs = got[(0,) * (got.ndim - 2) + (at,)].astype(F32)
    total = kept + got.astype(F32) * jnp.exp2(theirs).reshape((1,) * (got.ndim - 1) + (128,))
    return total, jnp.maximum(expo, theirs) + 1.0


def block_of(acc, *index):
    start = (*index, *(0,) * (acc.ndim - len(index)))
    block = lax.dynamic_slice(acc, start, (1,) * len(index) + acc.shape[len(index) :])
    return block.reshape(acc.shape[len(index) :])


def decode(got, at):
    theirs = got[(0,) * (got.ndim - 2) + (at,)].astype(F32)
    return got.astype(F32) * jnp.exp2(theirs).reshape((1,) * (got.ndim - 1) + (128,)), theirs


def reduction(acc, expo, at, z_dim):
    (first, send_first), (second, send_second), *rest = stages()
    ahead = encode(block_of(acc, 1 - first, 1 - second), expo, at)
    got_ahead = send_first(ahead)
    behind = encode(block_of(acc, 1 - first, second), expo, at)
    got_behind = send_first(behind)
    token = yield ahead, behind
    more, theirs = decode(after(got_ahead, token), at)
    expo = jnp.maximum(expo, theirs) + 1.0
    message = encode(block_of(acc, first, 1 - second) + more, expo, at)
    got = send_second(message)
    token = yield message
    got, got_behind = after((got, got_behind), token)
    more, theirs = decode(got, at)
    acc = block_of(acc, first, second) + decode(got_behind, at)[0] + more
    expo = jnp.maximum(expo, theirs) + 1.0
    acc = jnp.swapaxes(acc.reshape(2, 2, *acc.shape[z_dim:]), 0, 1)
    for mine, send in rest:
        message = encode(block_of(acc, 1 - mine), expo, at)
        got = send(message)
        token = yield message
        more, theirs = decode(after(got, token), at)
        acc, expo = block_of(acc, mine) + more, jnp.maximum(expo, theirs) + 1.0
    yield acc, expo


def gathering(piece, scale, core):
    (first, send_first), (second, send_second), *rest = stages()
    to_sibling = lambda a: flip(a, "mp", 0)
    wider = lambda a: a.astype(F32) * scale
    for mine, send in reversed(rest):
        other = send(piece)
        token = yield piece
        other = after(other, token)
        low = mine == 0
        piece = jnp.stack([jnp.where(low, piece, other), jnp.where(low, other, piece)], axis=0)
    by_second, by_first, sib = send_second(piece), send_first(piece), to_sibling(piece)
    every = [((core, first, second), wider(piece))]
    token = yield piece
    by_second = after(by_second, token)
    by_both, sib_second = send_first(by_second), to_sibling(by_second)
    by_first = after(by_first, by_second)
    sib_first = to_sibling(by_first)
    every.append(((core, first, 1 - second), wider(by_second)))
    every.append(((core, 1 - first, second), wider(by_first)))
    every.append(((1 - core, second, first), wider(after(sib, token))))
    token = yield [values for _, values in every]
    by_both = after(by_both, token)
    sib_both = to_sibling(by_both)
    every.append(((core, 1 - first, 1 - second), wider(by_both)))
    every.append(((1 - core, second, 1 - first), wider(sib_second)))
    every.append(((1 - core, 1 - second, first), wider(sib_first)))
    every.append(((1 - core, 1 - second, 1 - first), wider(sib_both)))
    yield every


def stages():
    return [
        (crossed_bit(0), lambda a: crossed_flip(a, 0)),
        (crossed_bit(1), lambda a: crossed_flip(a, 1)),
        (bit_of("dp", 1), lambda a: flip(a, "dp", 1)),
        (bit_of("dp", 2), lambda a: flip(a, "dp", 2)),
    ]


def assemble_kernel(rows, full, at_ref, *refs):
    pieces, (cross_ref, deep_ref, vec_ref) = refs[:8], refs[8:]
    hidden = deep_ref.shape[1]
    extra = full - hidden
    quarter = pieces[0].shape[2] - FRONT
    kinds = [
        (0, full, deep_ref, 0),
        (full, full + 1, vec_ref, 9),
        (rows, rows + full, cross_ref, 0),
        (rows + full, rows + full + 1, vec_ref, 8),
        (2 * rows + 8, 2 * rows + 16, vec_ref, 0),
    ]

    def turned(lines):
        lines = jnp.concatenate([lines, jnp.zeros((128 - lines.shape[0], 128), F32)], axis=0)
        return lines.T

    def copy(piece, q, core):
        for z in range(4):
            block = piece.at[z % 2, z // 2]
            lanes = pl.ds(pl.multiple_of((core * 4 + z) * 128, 128), 128)
            for first, end, out, base in kinds:
                lo, hi = max(first, q * quarter), min(end, (q + 1) * quarter)
                if lo < hi:
                    place = slice(base + lo - first, base + hi - first)
                    out[place, lanes] = block[FRONT + lo - q * quarter : FRONT + hi - q * quarter, :]
            if q == 3:
                over = FRONT + 2 * rows - q * quarter
                cross_ref[lanes, hidden:full] = turned(block[over : over + 8, :])[:, 0:extra]
                if z == 0:

                    @pl.when(core == 0)
                    def _():
                        corner = turned(block[over + 10 : over + 10 + extra, :])
                        cross_ref[hidden:full, hidden:full] = corner[0:extra, 0:extra]
                        vec_ref[8:9, hidden:full] = corner[extra : extra + 1, 0:extra]
                        vec_ref[0:1, hidden:full] = block[over + 13 : over + 14, 0:extra]

    for k, piece in enumerate(pieces):
        for q in range(4):
            pl.when(at_ref[k] == q)(lambda piece=piece, q=q, k=k: copy(piece, q, at_ref[8 + k]))


def assemble(pieces, rows, full, hidden):
    quarters = [jnp.where(c == 0, s * 2 + f, f * 2 + s) for (c, f, s), _ in pieces]
    at = jnp.stack([jnp.asarray(v, jnp.int32) for v in quarters + [c for (c, _, _), _ in pieces]])
    shape = jax.ShapeDtypeStruct
    return pl.pallas_call(
        lambda *refs: assemble_kernel(rows, full, *refs),
        in_specs=[pl.BlockSpec(memory_space=pltpu.SMEM)] + [pl.BlockSpec(memory_space=pltpu.VMEM)] * 8,
        out_shape=[shape((full, full), F32), shape((full, hidden), F32), shape((16, hidden + 128), F32)],
        compiler_params=params(14),
        cost_estimate=cost(0, 16 * rows * hidden),
        name="assemble",
    )(at, *[values for _, values in pieces])


def table_place(ids, table_rows, n_dp, core):
    upper = ids // (2 * table_rows)
    rest = ids % table_rows
    if n_dp == 8:
        piece = table_rows // n_dp
        at = rest // piece
        low = at % 2
        first = jnp.where(core == 0, low, upper)
        second = jnp.where(core == 0, upper, low)
        block = first * 4 + second * 2 + at // 4
        place = (at // 2) % 2 * piece + rest % piece
    else:
        block = upper * (table_rows // HI) + rest // HI
        place = rest % HI
    return place, jnp.where((ids // table_rows) % 2 == core, block, -1)


def body(
    field_ids,
    field_present,
    dense_values,
    dense_present,
    clicked,
    tables,
    cross_weight,
    cross_bias,
    deep_weight,
    deep_bias,
    head_cross,
    head_deep,
    head_bias,
):
    fields, batch_group = field_ids.shape
    table_rows, cat = tables.shape
    emb = cat // fields
    full, hidden = deep_weight.shape
    dense = full - cat
    n_dp, n_mp = lax.axis_size("dp"), lax.axis_size("mp")
    examples = batch_group // n_mp
    examples_all = batch_group * n_dp
    blocks = table_rows // HI
    rows = ceil_to(full + ONES, 8)
    me = lax.axis_index("mp")
    core = me & 1

    chosen = jnp.where(field_present > 0, field_ids, 0)
    own_ids = lax.dynamic_slice_in_dim(chosen, me * examples, examples, 1)
    place_own = own_ids & (HI - 1)
    block_own = (own_ids // HI) ^ (me * blocks)
    pair_ids = lax.dynamic_slice_in_dim(chosen, (me - core) * examples, 2 * examples, 1)
    place, block = table_place(pair_ids, table_rows, n_dp, core)

    columns = tables.T
    cuts = [(0, CUTS[0]), CUTS, (CUTS[1], fields)]
    far = [columns[a * emb : b * emb] for a, b in cuts[:2]]
    first_weight = after(cross_weight, far)
    weights = prepare(first_weight, deep_weight, cross_bias, deep_bias, head_cross, head_deep, rows)
    far.append(after(columns, weights[0])[cuts[2][0] * emb :])
    far = [flip(part, "mp", 1) for part in far]
    near = flip(columns, "mp", 0)
    place, block = after((place, block), weights[0])
    token = place, block
    found = []
    for k, (a, b) in enumerate(cuts):
        far_near = flip(after(far[k], token), "mp", 0)
        found.append(lookup(place_own[a:b], block_own[a:b], (columns, near, far[k], far_near), a * emb, emb))
        token = found[-1]

    logit, xa, grads, demb, dense_grad, hca, hda, sc, expo = layers(
        found,
        dense_values,
        dense_present,
        clicked[None, :],
        weights[:2],
        (*weights[2:], jnp.broadcast_to(head_bias[:, None], (8, 128))),
        emb,
        1.0 / math.sqrt(examples_all),
    )
    demb_sib = flip(demb, "mp", 0)
    grad_args = (xa, grads, hca, hda, sc, expo, examples_all)
    away, over = weight_grads(1 - core, *grad_args)
    if n_dp == 8:
        away = encode(away, expo[0], FRONT - 1)
    got = flip(away, "mp", 0)
    (sums,) = weight_grads(after(core, away), *grad_args, over)
    spans = [(0, 10), (10, fields)]

    def table_part(token, span, part, into=None):
        given = after(demb, token)
        values, top = spread(core, place, block, given, demb_sib, span, part, blocks, None if into is None else into[0])
        top = top[0] if into is None else jnp.maximum(top[0], into[1])
        return values, top

    if n_dp == 8:
        got = after(got, sums)
        both, expo = add(sums, expo[0], got, FRONT - 1)
        both = both.reshape(2, 2, *sums.shape[1:])
        weight_chain = reduction(both, expo, FRONT - 1, 1)
        token = next(weight_chain)
        table_chains = []
        for span in spans:
            part, top = table_part(token, span, span)
            part = part.reshape(2, 2, 2, 2, *part.shape[3:])
            table_chains.append(reduction(part, top, PAD - 1, 2))
            token = weight_chain.send(part)
            token = token, next(table_chains[-1])
        chain = {"w": weight_chain, "a": table_chains[0], "b": table_chains[1]}
        table_out, total = {}, None
        for name in "awbawwabwabwbw":
            token = chain[name].send(token)
            if name == "w" and total is None and isinstance(token, tuple):
                total, expo = token
                total = (total * jnp.exp2(-expo)[None, :]).astype(F16)
                chain["w"] = gathering(total, jnp.exp2(expo), core)
                token = next(chain["w"])
            elif name != "w" and isinstance(token, tuple):
                table_out[name] = token[0]
                if len(table_out) == 2:
                    tables_grad = jnp.concatenate([table_out["a"], table_out["b"]], axis=0)
                    token = tables_grad = tables_grad.reshape(fields, PAD, -1)[:, :emb].reshape(cat, -1)
                else:
                    token = token[0]
        pieces = token
    else:
        summed = lax.psum(sums + got, "dp")
        summed = summed + flip(summed, "mp", 1)
        pieces = lax.all_gather(summed, "mp")[0:2].reshape(2, 2, 2, 2, 2, *sums.shape[2:])
        pieces = jnp.swapaxes(pieces, 3, 4)
        pieces = [((c, f, s), pieces[c, f, s]) for c in range(2) for f in range(2) for s in range(2)]
        table_out = jnp.concatenate([table_part(sums, span, span)[0] for span in spans], axis=3)
        table_out = table_out.transpose(0, 3, 1, 2, 4).reshape(2, fields * PAD, table_rows)
        upper = bit_of("mp", 1)
        away = lax.dynamic_index_in_dim(table_out, 1 - upper, 0, keepdims=False)
        table_out = lax.dynamic_index_in_dim(table_out, upper, 0, keepdims=False) + flip(away, "mp", 1)
        table_out = lax.psum_scatter(table_out, "dp", scatter_dimension=1, tiled=True)
        tables_grad = table_out.reshape(fields, PAD, -1)[:, :emb].reshape(cat, -1)
    cross_grad, deep_grad, small = assemble(pieces, rows, full, hidden)
    return (
        logit[0],
        small[6, 0],
        dense_grad,
        tables_grad.T,
        cross_grad,
        small[8, 0:full],
        deep_grad,
        small[9, 0:hidden],
        small[0, 0:full],
        small[1, 0:hidden],
        small[6, 1:2],
    )


def solution(mesh):
    placed = (
        P(None, "dp"),
        P(None, "dp"),
        P(None, ("dp", "mp")),
        P(None, ("dp", "mp")),
        P(("dp", "mp")),
        P("mp", None),
        P(),
        P(),
        P(),
        P(),
        P(),
        P(),
        P(),
    )
    return jax.shard_map(
        body,
        mesh=mesh,
        in_specs=placed,
        out_specs=(
            P(("dp", "mp")),
            P(),
            P(None, ("dp", "mp")),
            P(("mp", "dp"), None),
            P(),
            P(),
            P(),
            P(),
            P(),
            P(),
            P(),
        ),
        check_vma=False,
    )
```
